256 devices in a mesh: row: 16 (over z, y_lo), col: 16 (over x, y_hi, core).
Axes of the slice: x: 4, y: 4 (y_hi: 2, y_lo: 2; y = y_hi * 2 + y_lo), z: 8, core: 2. Of those that a mesh axis runs over, the one named last changes fastest.
Arguments:
- features: bfloat16 [768, 8192], P('col', 'row'), may hold values from -6 to 6
- gate_weight: bfloat16 [8192, 14336], P('row', 'col'), may hold values from -0.0625 to 0.0625
- up_weight: bfloat16 [8192, 14336], P('row', 'col'), may hold values from -0.0625 to 0.0625
- down_weight: bfloat16 [14336, 8192], P('col', 'row'), may hold values from -0.046875 to 0.046875
- cotangent: bfloat16 [768, 8192], P('col', 'row'), may hold values from -6 to 6
Outputs:
- output: float32 [768, 8192], P('col', 'row')
- input_grad: float32 [768, 8192], P('col', 'row')
- gate_wgrad: float32 [8192, 14336], P('row', 'col')
- up_wgrad: float32 [8192, 14336], P('row', 'col')
- down_wgrad: float32 [14336, 8192], P('col', 'row')
The draws below stay inside these ranges and needn't reach their ends.
All inputs are finite; a program needn't handle non-finite values.
Results may differ from the reference program's by a relative error of at most 0.0029.
Values may be sent and summed in bfloat16 or wider, within the bound.
A program may use at most 64 MiB of HBM per device.

```python
import jax
import jax.numpy as jnp

D = 8192
FF = 14336
TOKENS = 768


def block_levels(own_key, dims, split, least, largest):
    factor_of = 1.0
    for axis_at, blocks in split:
        heights = jax.random.uniform(jax.random.fold_in(jax.random.fold_in(own_key, 6), axis_at), (blocks,), jnp.float32, least / len(split), largest / len(split))
        factor_of = factor_of * jnp.repeat(jnp.exp(heights), dims[axis_at] // blocks).reshape((-1,) + (1,) * (len(dims) - 1 - axis_at))
    return factor_of


def gaussian(key, dims, scale, limit, split=(), dtype=jnp.bfloat16):
    array = jax.random.normal(key, dims, jnp.float32) * scale
    if len(split) > 0:
        array = block_levels(key, dims, split, -0.22, 0.18) * array
    return jnp.clip(array, min=-limit, max=limit).astype(dtype)


def setup_inputs(seed: int = 0) -> dict:
    arg_keys = jax.random.split(jax.random.key(seed), 6)
    return {
        "features": gaussian(arg_keys[0], (TOKENS, D), 1.0, 6.0, ((0, 16), (1, 16))),
        "gate_weight": gaussian(arg_keys[1], (D, FF), D ** -0.5, 0.0625, ((0, 16), (1, 16))),
        "up_weight": gaussian(arg_keys[2], (D, FF), D ** -0.5, 0.0625, ((0, 16), (1, 16))),
        "down_weight": gaussian(arg_keys[3], (FF, D), FF ** -0.5, 0.046875, ((0, 16), (1, 16))),
        "cotangent": gaussian(arg_keys[4], (TOKENS, D), 1.0, 6.0, ((0, 16), (1, 16))),
    }


def reference(features, gate_weight, up_weight, down_weight, cotangent):
    gate_pre = jnp.dot(features, gate_weight, preferred_element_type=jnp.float32)
    up_pre = jnp.dot(features, up_weight, preferred_element_type=jnp.float32)
    sig = jax.nn.sigmoid(gate_pre)
    silu_gate = gate_pre * sig
    hidden = (silu_gate * up_pre).astype(jnp.bfloat16)
    output = jnp.dot(hidden, down_weight, preferred_element_type=jnp.float32)
    hid_grad = jnp.dot(cotangent, down_weight.T, preferred_element_type=jnp.float32)
    gate_grad = (hid_grad * up_pre * sig * (1.0 + gate_pre * (1.0 - sig))).astype(jnp.bfloat16)
    up_grad = (hid_grad * silu_gate).astype(jnp.bfloat16)
    input_grad = (jnp.dot(gate_grad, gate_weight.T, preferred_element_type=jnp.float32)
                  + jnp.dot(up_grad, up_weight.T, preferred_element_type=jnp.float32))
    gate_wgrad = jnp.dot(features.T, gate_grad, preferred_element_type=jnp.float32)
    up_wgrad = jnp.dot(features.T, up_grad, preferred_element_type=jnp.float32)
    down_wgrad = jnp.dot(hidden.T, cotangent, preferred_element_type=jnp.float32)
    return output, input_grad, gate_wgrad, up_wgrad, down_wgrad
```

```python
import jax
import jax.numpy as jnp
from jax import lax
from jax.experimental import pallas as pl
from jax.experimental.pallas import tpu as pltpu
from jax.sharding import PartitionSpec as P

MESH = pl.DeviceIdType.MESH
F32, BF16 = jnp.float32, jnp.bfloat16
NZ = 8
T = 48
D = 512
FA, FB = 512, 384
F = FA + FB
CA, CB = 3 * FA, 3 * FB
HALF = CA // 2
SCALE = 4096.0
CSCALE = 1024.0
ORDER = (4, 3, 5, 2, 6, 1, 7, 0)
POS = {off: at for at, off in enumerate(ORDER)}
BACK = (0, 1, 7, 2, 6, 3, 5, 4)
BPOS = {off: at for at, off in enumerate(BACK)}


def enc5(value):
    value = value * SCALE
    square = value * value
    return (square * square * value).astype(BF16)


def dec5(code):
    code = code.astype(F32)
    root = jnp.exp2(jnp.log2(jnp.abs(code)) * 0.2) * (1.0 / SCALE)
    return jnp.where(code < 0, -root, root)


def enc3(value):
    value = value * CSCALE
    return (value * value * value).astype(BF16)


def dec3(code):
    code = code.astype(F32)
    root = jnp.exp2(jnp.log2(jnp.abs(code)) * (1.0 / 3.0)) * (1.0 / CSCALE)
    return jnp.where(code < 0, -root, root)


def dot(left, right):
    return jnp.dot(left, right, preferred_element_type=F32)


def dot_t(left, right):
    return lax.dot_general(left, right, (((1,), (1,)), ((), ())), preferred_element_type=F32)


def rows(count, step=16):
    def run(fn):
        @pl.loop(0, count // step)
        def _(i):
            fn(pl.ds(pl.multiple_of(i * step, step), step))

    return run


def layer_kernel(
    x_hbm, g_hbm, u_hbm, d_hbm, c_hbm,
    out_ref, ing_ref, xc_hbm, ga_hbm, gb_hbm,
    g_w, u_w, d_w, xc, pa, pb, ya_s, ya_r, yb_s, yb_r, za_s, za_r, zb_s, zb_r,
    ga, gb, oi, sib_r, col_s, col_r,
    load_sem, ag_ss, ag_rs, fw_ss, fw_rs, ya_ss, ya_rs, yb_ss, yb_rs,
    za_ss, za_rs, zb_ss, zb_rs, gaz_ss, gaz_rs, gay_ss, gay_rs, gbz_ss, gbz_rs, gby_ss, gby_rs,
    sib_ss, sib_rs, col_ss, col_rs, store_sem,
):
    row, col = lax.axis_index("row"), lax.axis_index("col")
    z, yl = row // 2, row % 2
    chip, core = col // 2, col % 2
    x, yh = chip // 2, chip % 2

    def at_chip(k):
        return ((x + k // 2) % 4) * 2 + (yh + k % 2) % 2

    def from_chip(k):
        return ((x + 4 - k // 2) % 4) * 2 + (yh + k % 2) % 2

    up_z = ((z + 1) % NZ) * 2 + yl
    down_z = ((z + NZ - 1) % NZ) * 2 + yl
    mate = (z * 2 + 1 - yl, col)
    sibling = (row, chip * 2 + 1 - core)
    ring = ((up_z, col), (down_z, col))

    def send(src, dst, ss, rs, to):
        copy = pltpu.make_async_remote_copy(
            src_ref=src, dst_ref=dst, send_sem=ss, recv_sem=rs, device_id=to, device_id_type=MESH
        )
        copy.start()
        return copy

    sent = []

    loads = [
        pltpu.make_async_copy(x_hbm, xc.at[col, 0], load_sem.at[0]),
        pltpu.make_async_copy(c_hbm, xc.at[col, 1], load_sem.at[1]),
        pltpu.make_async_copy(g_hbm, g_w, load_sem.at[2]),
        pltpu.make_async_copy(u_hbm, u_w, load_sem.at[3]),
        pltpu.make_async_copy(d_hbm, d_w, load_sem.at[4]),
    ]
    for copy in loads:
        copy.start()

    barrier = pltpu.get_barrier_semaphore()
    for k in range(1, 8):
        pl.semaphore_signal(barrier, inc=1, device_id=(row, from_chip(k) * 2 + core), device_id_type=MESH)
    for to in (sibling, mate, ring[0], ring[1]):
        pl.semaphore_signal(barrier, inc=1, device_id=to, device_id_type=MESH)
    pl.semaphore_wait(barrier, 11)
    loads[0].wait()
    loads[1].wait()

    direct = []
    for k in (4, 5, 2, 6, 3, 7, 1):
        direct.append((k, send(xc.at[col], xc.at[col], ag_ss.at[k], ag_rs.at[k], (row, at_chip(k) * 2 + core))))
    forwarded = [send(xc.at[col], xc.at[col], fw_ss.at[0], fw_rs.at[0], sibling)]
    for k in (1, 2, 6, 3, 7, 4, 5):
        src = from_chip(k) * 2 + core
        pltpu.make_async_remote_copy(
            src_ref=xc.at[src], dst_ref=xc.at[src], send_sem=ag_ss.at[k], recv_sem=ag_rs.at[k],
            device_id=mate, device_id_type=MESH,
        ).wait_recv()
        forwarded.append(send(xc.at[src], xc.at[src], fw_ss.at[k], fw_rs.at[k], sibling))
    for copy in loads[2:]:
        copy.wait()
    for k, copy in enumerate(forwarded):
        copy.wait_recv()
    sent += [copy for _, copy in direct] + forwarded
    keep_xc = pltpu.make_async_copy(xc, xc_hbm, store_sem.at[0])
    keep_xc.start()

    def partial(at, off):
        piece = (z + off) % NZ

        def tokens(which):
            both = jnp.concatenate([xc[2 * piece + yl, which], xc[2 * piece + 1 - yl, which]], axis=0)
            return both

        feats, cots = tokens(0), tokens(1)
        pa[at, :, 0:FA] = dot(feats, g_w[:, 0:FA])
        pa[at, :, FA : 2 * FA] = dot(feats, u_w[:, 0:FA])
        pa[at, :, 2 * FA : CA] = dot_t(cots, d_w[0:FA, :])
        pb[at, :, 0:FB] = dot(feats, g_w[:, FA:F])
        pb[at, :, FB : 2 * FB] = dot(feats, u_w[:, FA:F])
        pb[at, :, 2 * FB : CB] = dot_t(cots, d_w[FA:F, :])

        @rows(T)
        def _(r):
            ya_s[at, r] = enc5(pa[at, pl.ds(pl.multiple_of(r.start + T, 16), 16)])

    def ya_send(at):
        return send(ya_s.at[at], ya_r.at[at], ya_ss.at[at], ya_rs.at[at], mate)

    def ya_wait(at):
        copy = pltpu.make_async_remote_copy(
            src_ref=ya_s.at[at], dst_ref=ya_r.at[at], send_sem=ya_ss.at[at], recv_sem=ya_rs.at[at],
            device_id=mate, device_id_type=MESH,
        )
        copy.wait_recv()
        return copy

    def za_part(way, step):
        if step:
            return (way, step)
        return (way, step, slice(None), pl.ds(way * HALF, HALF))

    def zb_part(way, step):
        if step:
            return (way, step)
        return (way, step, pl.ds(way * T, T))

    def za_send(way, step):
        part = za_part(way, step)
        copy = send(za_s.at[part], za_r.at[part], za_ss.at[way, step], za_rs.at[way, step], ring[way])
        sent.append(copy)
        return copy

    def zb_send(way, step):
        part = zb_part(way, step)
        copy = send(zb_s.at[part], zb_r.at[part], zb_ss.at[way, step], zb_rs.at[way, step], ring[way])
        sent.append(copy)
        return copy

    partial(0, 4)
    ya_send(0)
    for way in range(2):
        @rows(T)
        def _(r, way=way):
            zb_s[way, 0, pl.ds(pl.multiple_of(r.start + way * T, 16), 16)] = enc5(
                pb[0, pl.ds(pl.multiple_of(r.start + way * T, 16), 16)]
            )

    zb_moves = {(way, 0): zb_send(way, 0) for way in range(2)}

    @pl.loop(1, NZ)
    def _(at):
        off = jnp.where(at % 2 == 1, 4 - (at + 1) // 2, 4 + at // 2)
        partial(at, off)
        ya_send(at)

    ya_wait(0)
    for way in range(2):
        cols = pl.ds(way * HALF, HALF)

        @rows(T)
        def _(r, cols=cols, way=way):
            za_s[way, 0, r, cols] = enc5(pa[0, r, cols] + dec5(ya_r[0, r, cols]))

    za_moves = {(way, 0): za_send(way, 0) for way in range(2)}

    for step in range(1, 4):
        for way in range(2):
            at = POS[4 - step if way == 0 else 4 + step]
            zb_moves[way, step - 1].wait_recv()
            if step == 1:
                got = way * T

                @rows(T)
                def _(r, got=got, at=at, way=way):
                    r1 = pl.ds(pl.multiple_of(r.start + got, 16), 16)
                    zb_s[way, 1, r1] = enc5(pb[at, r1] + dec5(zb_r[way, 0, r1]))
                    r2 = pl.ds(pl.multiple_of(r.start + (T - got), 16), 16)
                    zb_s[way, 1, r2] = enc5(pb[at, r2])
            else:

                @rows(2 * T)
                def _(r, at=at, way=way, step=step):
                    zb_s[way, step, r] = enc5(pb[at, r] + dec5(zb_r[way, step - 1, r]))

            zb_moves[way, step] = zb_send(way, step)
        for way in range(2):
            at = POS[4 - step if way == 0 else 4 + step]
            ya_wait(at)
            za_moves[way, step - 1].wait_recv()
            if step == 1:
                got = pl.ds(way * HALF, HALF)
                rest = pl.ds((1 - way) * HALF, HALF)

                @rows(T)
                def _(r, got=got, rest=rest, at=at, way=way):
                    za_s[way, 1, r, got] = enc5(
                        pa[at, r, got] + dec5(ya_r[at, r, got]) + dec5(za_r[way, 0, r, got])
                    )
                    za_s[way, 1, r, rest] = enc5(pa[at, r, rest] + dec5(ya_r[at, r, rest]))
            else:

                @rows(T)
                def _(r, at=at, way=way, step=step):
                    za_s[way, step, r] = enc5(
                        pa[at, r] + dec5(ya_r[at, r]) + dec5(za_r[way, step - 1, r])
                    )

            za_moves[way, step] = za_send(way, step)

    for way in range(2):
        zb_moves[way, 3].wait_recv()

    @rows(T)
    def _(r):
        r2 = pl.ds(pl.multiple_of(r.start + T, 16), 16)
        yb_s[r] = enc5(pb[7, r2] + dec5(zb_r[0, 3, r2]) + dec5(zb_r[1, 3, r2]))

    yb_move = send(yb_s, yb_r, yb_ss, yb_rs, mate)
    sent.append(yb_move)

    def activate(gate, up, hid):
        sig = jax.nn.sigmoid(gate)
        silu = gate * sig
        return (
            (silu * up).astype(BF16),
            (hid * up * sig * (1.0 + gate * (1.0 - sig))).astype(BF16),
            (hid * silu).astype(BF16),
        )

    ya_wait(7)
    for way in range(2):
        za_moves[way, 3].wait_recv()

    @rows(T)
    def _(r):
        def total(first):
            cols = pl.ds(first, FA)
            return pa[7, r, cols] + dec5(ya_r[7, r, cols]) + dec5(za_r[0, 3, r, cols]) + dec5(za_r[1, 3, r, cols])

        hidden, gate_grad, up_grad = activate(total(0), total(FA), total(2 * FA))
        ga[row, r, 0:FA] = hidden
        ga[row, r, FA : 2 * FA] = gate_grad
        ga[row, r, 2 * FA : CA] = up_grad

    def gaz_send(way, step):
        src = ((z + NZ - step) % NZ if way == 0 else (z + step) % NZ) * 2 + yl
        if step < 3:
            part = ga.at[src]
        else:
            part = ga.at[src, :, pl.ds(way * HALF, HALF)]
        copy = send(part, part, gaz_ss.at[way, step], gaz_rs.at[way, step], ring[way])
        sent.append(copy)

    def gaz_wait(way, step):
        src = ((z + NZ - 1 - step) % NZ if way == 0 else (z + step + 1) % NZ) * 2 + yl
        if step < 3:
            part = ga.at[src]
        else:
            part = ga.at[src, :, pl.ds(way * HALF, HALF)]
        pltpu.make_async_remote_copy(
            src_ref=part, dst_ref=part, send_sem=gaz_ss.at[way, step], recv_sem=gaz_rs.at[way, step],
            device_id=mate, device_id_type=MESH,
        ).wait_recv()

    def gay_send(off):
        part = ga.at[((z + off) % NZ) * 2 + yl]
        sent.append(send(part, part, gay_ss.at[off], gay_rs.at[off], mate))

    def gay_wait(off):
        part = ga.at[((z + off) % NZ) * 2 + 1 - yl]
        pltpu.make_async_remote_copy(
            src_ref=part, dst_ref=part, send_sem=gay_ss.at[off], recv_sem=gay_rs.at[off],
            device_id=mate, device_id_type=MESH,
        ).wait_recv()

    def gbz_part(way, step, src):
        if step < 3:
            return gb.at[pl.ds(2 * src, 2)]
        return gb.at[2 * src + way]

    def gbz_send(way, step):
        part = gbz_part(way, step, (z + NZ - step) % NZ if way == 0 else (z + step) % NZ)
        sent.append(send(part, part, gbz_ss.at[way, step], gbz_rs.at[way, step], ring[way]))

    def gbz_wait(way, step):
        part = gbz_part(way, step, (z + NZ - 1 - step) % NZ if way == 0 else (z + step + 1) % NZ)
        pltpu.make_async_remote_copy(
            src_ref=part, dst_ref=part, send_sem=gbz_ss.at[way, step], recv_sem=gbz_rs.at[way, step],
            device_id=mate, device_id_type=MESH,
        ).wait_recv()

    for way in range(2):
        gaz_send(way, 0)
    yb_move.wait_recv()

    @rows(T)
    def _(r):
        def total(first):
            cols = pl.ds(first, FB)
            return (
                pb[7, r, cols] + dec5(zb_r[0, 3, r, cols]) + dec5(zb_r[1, 3, r, cols]) + dec5(yb_r[r, cols])
            )

        hidden, gate_grad, up_grad = activate(total(0), total(FB), total(2 * FB))
        gb[row, r, 0:FB] = hidden
        gb[row, r, FB : 2 * FB] = gate_grad
        gb[row, r, 2 * FB : CB] = up_grad

    part = gb.at[row]
    sent.append(send(part, part, gby_ss, gby_rs, mate))
    gay_send(0)

    def products(at, off):
        piece = (z + off) % NZ
        both = pl.ds(2 * piece, 2)

        def part(ref, first, width):
            return ref[both, :, first : first + width].reshape(2 * T, width)

        outs = dot(part(ga, 0, FA), d_w[0:FA, :]) + dot(part(gb, 0, FB), d_w[FA:F, :])
        grads = (
            dot_t(part(ga, FA, FA), g_w[:, 0:FA])
            + dot_t(part(ga, 2 * FA, FA), u_w[:, 0:FA])
            + dot_t(part(gb, FB, FB), g_w[:, FA:F])
            + dot_t(part(gb, 2 * FB, FB), u_w[:, FA:F])
        )
        oi[at, :, :, 0:D] = outs.reshape(2, T, D)
        oi[at, :, :, D : 2 * D] = grads.reshape(2, T, D)
        send(oi.at[at, 1 - core], sib_r.at[at], sib_ss.at[at], sib_rs.at[at], sibling)

    def sib_copy(at):
        return pltpu.make_async_remote_copy(
            src_ref=oi.at[at, 1 - core], dst_ref=sib_r.at[at], send_sem=sib_ss.at[at], recv_sem=sib_rs.at[at],
            device_id=sibling, device_id_type=MESH,
        )

    def col_copy(at, k, to):
        return pltpu.make_async_remote_copy(
            src_ref=col_s.at[at], dst_ref=col_r.at[k], send_sem=col_ss.at[k], recv_sem=col_rs.at[k],
            device_id=(row, to * 2 + core), device_id_type=MESH,
        )

    def reduce_to_owner(at, off):
        piece = (z + off) % NZ
        sib_copy(at).wait_recv()

        @pl.when(piece == chip)
        def _():
            out_ref[...] = oi[at, core, :, 0:D] + sib_r[at, :, 0:D]
            ing_ref[...] = oi[at, core, :, D : 2 * D] + sib_r[at, :, D : 2 * D]

        @pl.when(piece != chip)
        def _():
            @rows(T)
            def _(r):
                col_s[at, r] = enc3(oi[at, core, r] + sib_r[at, r])

            k = ((piece // 2 + 4 - x) % 4) * 2 + (piece + yh) % 2
            col_copy(at, k, piece).start()

    gby = gb.at[mate[0]]
    pltpu.make_async_remote_copy(
        src_ref=gby, dst_ref=gby, send_sem=gby_ss, recv_sem=gby_rs, device_id=mate, device_id_type=MESH
    ).wait_recv()
    for way in range(2):
        gbz_send(way, 0)

    def offs_of(step):
        return (NZ - 1 - step, step + 1)

    for step in range(4):
        for way in range(2):
            gaz_wait(way, step)
            if step < 3:
                gaz_send(way, step + 1)
                gay_send(offs_of(step)[way])
        if step == 3:
            gay_send(4)
        if step == 0:
            gay_wait(0)
            products(0, 0)
        else:
            for way in range(2):
                off = offs_of(step - 1)[way]
                gay_wait(off)
                products(BPOS[off], off)
        for way in range(2):
            gbz_wait(way, step)
            if step < 3:
                gbz_send(way, step + 1)
        if step == 0:
            reduce_to_owner(0, 0)
        else:
            for way in range(2):
                off = offs_of(step - 1)[way]
                reduce_to_owner(BPOS[off], off)

    gay_wait(4)
    products(7, 4)
    keep_ga = pltpu.make_async_copy(ga, ga_hbm, store_sem.at[1])
    keep_gb = pltpu.make_async_copy(gb, gb_hbm, store_sem.at[2])
    keep_ga.start()
    keep_gb.start()
    reduce_to_owner(7, 4)
    for k in range(1, 8):
        col_copy(0, k, at_chip(k)).wait_recv()

        @rows(T)
        def _(r, k=k):
            out_ref[r] += dec3(col_r[k, r, 0:D])
            ing_ref[r] += dec3(col_r[k, r, D : 2 * D])

    for copy in sent:
        copy.wait_send()

    @pl.loop(0, NZ)
    def _(at):
        pltpu.make_async_remote_copy(
            src_ref=ya_s.at[at], dst_ref=ya_r.at[at], send_sem=ya_ss.at[at], recv_sem=ya_rs.at[at],
            device_id=mate, device_id_type=MESH,
        ).wait_send()
        sib_copy(at).wait_send()

    for k in range(1, 8):
        col_copy(0, k, at_chip(k)).wait_send()
    keep_xc.wait()
    keep_ga.wait()
    keep_gb.wait()


def layer(features, gate_weight, up_weight, down_weight, cotangent):
    vmem = pltpu.VMEM
    dma = pltpu.SemaphoreType.DMA
    hbm = pl.BlockSpec(memory_space=pl.ANY)
    full = pl.BlockSpec(memory_space=pltpu.VMEM)
    return pl.pallas_call(
        layer_kernel,
        out_shape=(
            jax.ShapeDtypeStruct((T, D), F32),
            jax.ShapeDtypeStruct((T, D), F32),
            jax.ShapeDtypeStruct((16, 2, T, D), BF16),
            jax.ShapeDtypeStruct((16, T, CA), BF16),
            jax.ShapeDtypeStruct((16, T, CB), BF16),
        ),
        in_specs=[hbm] * 5,
        out_specs=(full, full, hbm, hbm, hbm),
        scratch_shapes=[
            vmem((D, F), BF16),
            vmem((D, F), BF16),
            vmem((F, D), BF16),
            vmem((16, 2, T, D), BF16),
            vmem((NZ, 2 * T, CA), F32),
            vmem((NZ, 2 * T, CB), F32),
            vmem((NZ, T, CA), BF16),
            vmem((NZ, T, CA), BF16),
            vmem((T, CB), BF16),
            vmem((T, CB), BF16),
            vmem((2, 4, T, CA), BF16),
            vmem((2, 4, T, CA), BF16),
            vmem((2, 4, 2 * T, CB), BF16),
            vmem((2, 4, 2 * T, CB), BF16),
            vmem((16, T, CA), BF16),
            vmem((16, T, CB), BF16),
            vmem((NZ, 2, T, 2 * D), F32),
            vmem((NZ, T, 2 * D), F32),
            vmem((NZ, T, 2 * D), BF16),
            vmem((NZ, T, 2 * D), BF16),
            dma((5,)),
            dma((8,)), dma((8,)), dma((8,)), dma((8,)),
            dma((8,)), dma((8,)), dma, dma,
            dma((2, 4)), dma((2, 4)), dma((2, 4)), dma((2, 4)),
            dma((2, 4)), dma((2, 4)), dma((8,)), dma((8,)),
            dma((2, 4)), dma((2, 4)), dma, dma,
            dma((8,)), dma((8,)), dma((8,)), dma((8,)),
            dma((3,)),
        ],
        compiler_params=pltpu.CompilerParams(
            collective_id=0, has_side_effects=True, vmem_limit_bytes=50 * 1024 * 1024
        ),
        name="layer",
    )(features, gate_weight, up_weight, down_weight, cotangent)


def wgrad_kernel(xc_ref, ga_ref, gb_ref, g_out, u_out, d_out):
    tokens = 16 * T
    over = (((0,), (0,)), ((), ()))

    def product(left, right):
        return lax.dot_general(left, right, over, preferred_element_type=F32)

    feats = xc_ref[:, 0].reshape(tokens, D)
    cots = xc_ref[:, 1].reshape(tokens, D)
    for ref, width, first in ((ga_ref, FA, 0), (gb_ref, FB, FA)):
        hidden = ref[:, :, 0:width].reshape(tokens, width)
        d_out[first : first + width, :] = product(hidden, cots)
        g_out[:, first : first + width] = product(feats, ref[:, :, width : 2 * width].reshape(tokens, width))
        u_out[:, first : first + width] = product(feats, ref[:, :, 2 * width : 3 * width].reshape(tokens, width))


def wgrads(xc, ga, gb):
    return pl.pallas_call(
        wgrad_kernel,
        out_shape=(
            jax.ShapeDtypeStruct((D, F), F32),
            jax.ShapeDtypeStruct((D, F), F32),
            jax.ShapeDtypeStruct((F, D), F32),
        ),
        compiler_params=pltpu.CompilerParams(vmem_limit_bytes=50 * 1024 * 1024),
        name="wgrads",
    )(xc, ga, gb)


def body(features, gate_weight, up_weight, down_weight, cotangent):
    output, input_grad, xc, ga, gb = layer(features, gate_weight, up_weight, down_weight, cotangent)
    gate_wgrad, up_wgrad, down_wgrad = wgrads(xc, ga, gb)
    return (output, input_grad, gate_wgrad, up_wgrad, down_wgrad)


def solution(mesh):
    in_specs = (P("col", "row"), P("row", "col"), P("row", "col"), P("col", "row"), P("col", "row"))
    out_specs = (
        P("col", "row"),
        P("col", "row"),
        P("row", "col"),
        P("row", "col"),
        P("col", "row"),
    )
    return jax.shard_map(body, mesh=mesh, in_specs=in_specs, out_specs=out_specs, check_vma=False)
```

```python
import jax
import jax.numpy as jnp
from jax import lax
from jax.experimental import pallas as pl
from jax.experimental.pallas import tpu as pltpu
from jax.sharding import PartitionSpec as P

MESH = pl.DeviceIdType.MESH
F32, BF16 = jnp.float32, jnp.bfloat16
NZ = 8
T = 48
D = 512
FA, FB = 512, 384
F = FA + FB
CA, CB = 3 * FA, 3 * FB
HALF = CA // 2
SCALE = 4096.0
CSCALE = 1024.0
ORDER = (4, 3, 5, 2, 6, 1, 7, 0)
POS = {off: at for at, off in enumerate(ORDER)}
BACK = (0, 1, 7, 2, 6, 3, 5, 4)
BPOS = {off: at for at, off in enumerate(BACK)}


def enc5(value):
    value = value * SCALE
    square = value * value
    return (square * square * value).astype(BF16)


def dec5(code):
    code = code.astype(F32)
    root = jnp.exp2(jnp.log2(jnp.abs(code)) * 0.2) * (1.0 / SCALE)
    return jnp.where(code < 0, -root, root)


def enc3(value):
    value = value * CSCALE
    return (value * value * value).astype(BF16)


def dec3(code):
    code = code.astype(F32)
    root = jnp.exp2(jnp.log2(jnp.abs(code)) * (1.0 / 3.0)) * (1.0 / CSCALE)
    return jnp.where(code < 0, -root, root)


def dot(left, right):
    return jnp.dot(left, right, preferred_element_type=F32)


def dot_t(left, right):
    return lax.dot_general(left, right, (((1,), (1,)), ((), ())), preferred_element_type=F32)


def rows(count, step=16):
    def run(fn):
        @pl.loop(0, count // step)
        def _(i):
            fn(pl.ds(pl.multiple_of(i * step, step), step))

    return run


def layer_kernel(
    x_hbm, g_hbm, u_hbm, d_hbm, c_hbm,
    out_ref, ing_ref, g_out, u_out, d_out,
    g_w, u_w, d_w, xf, xc, ft, pa, pb, ya_s, ya_r, yb_s, yb_r, za_s, za_r, zb_s, zb_r,
    ga, gb, oi, sib_r, col_s, col_r, acc, fin_s, fin_r,
    load_sem, f_ss, f_rs, c_ss, c_rs, ff_ss, ff_rs, cf_ss, cf_rs, ya_ss, ya_rs, yb_ss, yb_rs,
    za_ss, za_rs, zb_ss, zb_rs, zh_ss, zh_rs, gaz_ss, gaz_rs, gay_ss, gay_rs, gbz_ss, gbz_rs, gby_ss, gby_rs,
    sib_ss, sib_rs, col_ss, col_rs, fin_ss, fin_rs,
):
    row, col = lax.axis_index("row"), lax.axis_index("col")
    z, yl = row // 2, row % 2
    chip, core = col // 2, col % 2
    x, yh = chip // 2, chip % 2

    def at_chip(k):
        return ((x + k // 2) % 4) * 2 + (yh + k % 2) % 2

    def from_chip(k):
        return ((x + 4 - k // 2) % 4) * 2 + (yh + k % 2) % 2

    up_z = ((z + 1) % NZ) * 2 + yl
    down_z = ((z + NZ - 1) % NZ) * 2 + yl
    mate = (z * 2 + 1 - yl, col)
    sibling = (row, chip * 2 + 1 - core)
    ring = ((up_z, col), (down_z, col))

    def send(src, dst, ss, rs, to):
        copy = pltpu.make_async_remote_copy(
            src_ref=src, dst_ref=dst, send_sem=ss, recv_sem=rs, device_id=to, device_id_type=MESH
        )
        copy.start()
        return copy

    sent = []

    loads = [
        pltpu.make_async_copy(x_hbm, xf.at[col], load_sem.at[0]),
        pltpu.make_async_copy(c_hbm, xc.at[col], load_sem.at[1]),
        pltpu.make_async_copy(g_hbm, g_w, load_sem.at[2]),
        pltpu.make_async_copy(u_hbm, u_w, load_sem.at[3]),
        pltpu.make_async_copy(d_hbm, d_w, load_sem.at[4]),
    ]
    for copy in loads:
        copy.start()

    barrier = pltpu.get_barrier_semaphore()
    for k in range(1, 8):
        pl.semaphore_signal(barrier, inc=1, device_id=(row, from_chip(k) * 2 + core), device_id_type=MESH)
    for to in (sibling, mate, ring[0], ring[1]):
        pl.semaphore_signal(barrier, inc=1, device_id=to, device_id_type=MESH)
    pl.semaphore_wait(barrier, 11)
    loads[0].wait()
    loads[1].wait()

    def arrival(ref, ss, rs):
        return pltpu.make_async_remote_copy(
            src_ref=ref, dst_ref=ref, send_sem=ss, recv_sem=rs, device_id=mate, device_id_type=MESH
        )

    def same_core(k):
        return (row, at_chip(k) * 2 + core)

    mine_f, mine_c = xf.at[col], xc.at[col]
    for k in (4, 5, 2, 6, 3, 7, 1):
        sent.append(send(mine_f, mine_f, f_ss.at[k], f_rs.at[k], same_core(k)))
    sent.append(send(mine_f, mine_f, ff_ss.at[0], ff_rs.at[0], sibling))
    for k in (1, 4, 2, 6):
        sent.append(send(mine_c, mine_c, c_ss.at[k], c_rs.at[k], same_core(k)))
    sent.append(send(mine_c, mine_c, cf_ss.at[0], cf_rs.at[0], sibling))

    def pass_on(ref, ss, rs, to_ss, to_rs, k):
        part = ref.at[from_chip(k) * 2 + core]
        arrival(part, ss.at[k], rs.at[k]).wait_recv()
        sent.append(send(part, part, to_ss.at[k], to_rs.at[k], sibling))

    for k in (1, 2, 6, 3, 7, 4, 5):
        pass_on(xf, f_ss, f_rs, ff_ss, ff_rs, k)
    pass_on(xc, c_ss, c_rs, cf_ss, cf_rs, 1)
    partner = xc.at[from_chip(1) * 2 + core]
    for k in (5, 3, 7):
        sent.append(send(partner, partner, c_ss.at[k], c_rs.at[k], same_core(k - 1)))
    for copy in loads[2:]:
        copy.wait()
    for k in range(8):
        arrival(mine_f, ff_ss.at[k], ff_rs.at[k]).wait_recv()

    def tokens(ref, off):
        piece = (z + off) % NZ
        return jnp.concatenate([ref[2 * piece + yl], ref[2 * piece + 1 - yl]], axis=0)

    def mates(r):
        return pl.ds(pl.multiple_of(r.start + T, 16), 16)

    def partial_gu(at, off):
        feats = tokens(xf, off)
        pa[at, :, 0:FA] = dot(feats, g_w[:, 0:FA])
        pa[at, :, FA : 2 * FA] = dot(feats, u_w[:, 0:FA])
        pb[at, :, 0:FB] = dot(feats, g_w[:, FA:F])
        pb[at, :, FB : 2 * FB] = dot(feats, u_w[:, FA:F])

        @rows(T)
        def _(r):
            ya_s[at, r, 0 : 2 * FA] = enc5(pa[at, mates(r), 0 : 2 * FA])

    def partial_h(at, off):
        cots = tokens(xc, off)
        pa[at, :, 2 * FA : CA] = dot_t(cots, d_w[0:FA, :])
        pb[at, :, 2 * FB : CB] = dot_t(cots, d_w[FA:F, :])

        @rows(T)
        def _(r):
            ya_s[at, r, 2 * FA : CA] = enc5(pa[at, mates(r), 2 * FA : CA])

    YA_COLS = (pl.ds(0, 2 * FA), pl.ds(2 * FA, FA))
    ZB_COLS = (pl.ds(0, 2 * FB), pl.ds(2 * FB, FB))

    def ya_copy(at, which):
        cols = YA_COLS[which]
        return pltpu.make_async_remote_copy(
            src_ref=ya_s.at[at, :, cols], dst_ref=ya_r.at[at, :, cols],
            send_sem=ya_ss.at[at, which], recv_sem=ya_rs.at[at, which],
            device_id=mate, device_id_type=MESH,
        )

    def ya_wait(at):
        for which in range(2):
            ya_copy(at, which).wait_recv()

    def za_part(way, step):
        if step:
            return (way, step)
        return (way, step, slice(None), pl.ds(way * HALF, HALF))

    def za_send(way, step):
        part = za_part(way, step)
        copy = send(za_s.at[part], za_r.at[part], za_ss.at[way, step], za_rs.at[way, step], ring[way])
        sent.append(copy)
        return copy

    def zb_send(way, step):
        part = (way, step)
        copy = send(zb_s.at[part], zb_r.at[part], zb_ss.at[way, step], zb_rs.at[way, step], ring[way])
        sent.append(copy)
        return copy

    def off_at(at):
        return jnp.where(at % 2 == 1, 4 - (at + 1) // 2, 4 + at // 2)

    zb_moves = {}
    zh_moves = {}

    def zb_first(which):
        cols = ZB_COLS[which]
        for way in range(2):
            @rows(T)
            def _(r, way=way):
                r2 = pl.ds(pl.multiple_of(r.start + way * T, 16), 16)
                zb_s[way, 0, r2, cols] = enc5(pb[0, r2, cols])

            part = (way, 0, pl.ds(way * T, T), cols)
            ss, rs = ((zb_ss, zb_rs), (zh_ss, zh_rs))[which]
            at = (way, 0) if which == 0 else way
            copy = send(zb_s.at[part], zb_r.at[part], ss.at[at], rs.at[at], ring[way])
            sent.append(copy)
            if which == 0:
                zb_moves[way, 0] = copy
            else:
                zh_moves[way] = copy

    partial_gu(0, 4)
    ya_copy(0, 0).start()
    zb_first(0)

    @pl.loop(1, 3)
    def _(at):
        partial_gu(at, off_at(at))
        ya_copy(at, 0).start()

    for k in (2, 6, 4, 3, 7, 5):
        pass_on(xc, c_ss, c_rs, cf_ss, cf_rs, k)

    @pl.loop(3, NZ)
    def _(at):
        partial_gu(at, off_at(at))

    for k in range(8):
        arrival(mine_c, cf_ss.at[k], cf_rs.at[k]).wait_recv()
    partial_h(0, 4)
    ya_copy(0, 1).start()
    zb_first(1)

    @pl.loop(1, 3)
    def _(at):
        partial_h(at, off_at(at))
        ya_copy(at, 1).start()

    @pl.loop(3, NZ)
    def _(at):
        partial_h(at, off_at(at))
        ya_copy(at, 0).start()
        ya_copy(at, 1).start()

    ft[...] = xf[...].reshape(16 * T, D).T

    ya_wait(0)
    for way in range(2):
        cols = pl.ds(way * HALF, HALF)

        @rows(T)
        def _(r, cols=cols, way=way):
            za_s[way, 0, r, cols] = enc5(pa[0, r, cols] + dec5(ya_r[0, r, cols]))

    za_moves = {(way, 0): za_send(way, 0) for way in range(2)}

    for step in range(1, 4):
        for way in range(2):
            at = POS[4 - step if way == 0 else 4 + step]
            zb_moves[way, step - 1].wait_recv()
            if step == 1:
                zh_moves[way].wait_recv()
                got = way * T

                @rows(T)
                def _(r, got=got, at=at, way=way):
                    r1 = pl.ds(pl.multiple_of(r.start + got, 16), 16)
                    zb_s[way, 1, r1] = enc5(pb[at, r1] + dec5(zb_r[way, 0, r1]))
                    r2 = pl.ds(pl.multiple_of(r.start + (T - got), 16), 16)
                    zb_s[way, 1, r2] = enc5(pb[at, r2])
            else:

                @rows(2 * T)
                def _(r, at=at, way=way, step=step):
                    zb_s[way, step, r] = enc5(pb[at, r] + dec5(zb_r[way, step - 1, r]))

            zb_moves[way, step] = zb_send(way, step)
        for way in range(2):
            at = POS[4 - step if way == 0 else 4 + step]
            ya_wait(at)
            za_moves[way, step - 1].wait_recv()
            if step == 1:
                got = pl.ds(way * HALF, HALF)
                rest = pl.ds((1 - way) * HALF, HALF)

                @rows(T)
                def _(r, got=got, rest=rest, at=at, way=way):
                    za_s[way, 1, r, got] = enc5(
                        pa[at, r, got] + dec5(ya_r[at, r, got]) + dec5(za_r[way, 0, r, got])
                    )
                    za_s[way, 1, r, rest] = enc5(pa[at, r, rest] + dec5(ya_r[at, r, rest]))
            else:

                @rows(T)
                def _(r, at=at, way=way, step=step):
                    za_s[way, step, r] = enc5(
                        pa[at, r] + dec5(ya_r[at, r]) + dec5(za_r[way, step - 1, r])
                    )

            za_moves[way, step] = za_send(way, step)

    for way in range(2):
        zb_moves[way, 3].wait_recv()

    @rows(T)
    def _(r):
        r2 = pl.ds(pl.multiple_of(r.start + T, 16), 16)
        yb_s[r] = enc5(pb[7, r2] + dec5(zb_r[0, 3, r2]) + dec5(zb_r[1, 3, r2]))

    yb_move = send(yb_s, yb_r, yb_ss, yb_rs, mate)
    sent.append(yb_move)

    def activate(gate, up, hid):
        sig = jax.nn.sigmoid(gate)
        silu = gate * sig
        return (
            (silu * up).astype(BF16),
            (hid * up * sig * (1.0 + gate * (1.0 - sig))).astype(BF16),
            (hid * silu).astype(BF16),
        )

    ya_wait(7)
    for way in range(2):
        za_moves[way, 3].wait_recv()

    @rows(T)
    def _(r):
        def total(first):
            cols = pl.ds(first, FA)
            return pa[7, r, cols] + dec5(ya_r[7, r, cols]) + dec5(za_r[0, 3, r, cols]) + dec5(za_r[1, 3, r, cols])

        hidden, gate_grad, up_grad = activate(total(0), total(FA), total(2 * FA))
        ga[row, r, 0:FA] = hidden
        ga[row, r, FA : 2 * FA] = gate_grad
        ga[row, r, 2 * FA : CA] = up_grad

    def gaz_send(way, step):
        src = ((z + NZ - step) % NZ if way == 0 else (z + step) % NZ) * 2 + yl
        if step < 3:
            part = ga.at[src]
        else:
            part = ga.at[src, :, pl.ds(way * HALF, HALF)]
        copy = send(part, part, gaz_ss.at[way, step], gaz_rs.at[way, step], ring[way])
        sent.append(copy)

    def gaz_wait(way, step):
        src = ((z + NZ - 1 - step) % NZ if way == 0 else (z + step + 1) % NZ) * 2 + yl
        if step < 3:
            part = ga.at[src]
        else:
            part = ga.at[src, :, pl.ds(way * HALF, HALF)]
        pltpu.make_async_remote_copy(
            src_ref=part, dst_ref=part, send_sem=gaz_ss.at[way, step], recv_sem=gaz_rs.at[way, step],
            device_id=mate, device_id_type=MESH,
        ).wait_recv()

    def gay_send(off):
        part = ga.at[((z + off) % NZ) * 2 + yl]
        sent.append(send(part, part, gay_ss.at[off], gay_rs.at[off], mate))

    def gay_wait(off):
        part = ga.at[((z + off) % NZ) * 2 + 1 - yl]
        pltpu.make_async_remote_copy(
            src_ref=part, dst_ref=part, send_sem=gay_ss.at[off], recv_sem=gay_rs.at[off],
            device_id=mate, device_id_type=MESH,
        ).wait_recv()

    def gbz_part(way, step, src):
        if step < 3:
            return gb.at[pl.ds(2 * src, 2)]
        return gb.at[2 * src + way]

    def gbz_send(way, step):
        part = gbz_part(way, step, (z + NZ - step) % NZ if way == 0 else (z + step) % NZ)
        sent.append(send(part, part, gbz_ss.at[way, step], gbz_rs.at[way, step], ring[way]))

    def gbz_wait(way, step):
        part = gbz_part(way, step, (z + NZ - 1 - step) % NZ if way == 0 else (z + step + 1) % NZ)
        pltpu.make_async_remote_copy(
            src_ref=part, dst_ref=part, send_sem=gbz_ss.at[way, step], recv_sem=gbz_rs.at[way, step],
            device_id=mate, device_id_type=MESH,
        ).wait_recv()

    for way in range(2):
        gaz_send(way, 0)
    yb_move.wait_recv()

    @rows(T)
    def _(r):
        def total(first):
            cols = pl.ds(first, FB)
            return (
                pb[7, r, cols] + dec5(zb_r[0, 3, r, cols]) + dec5(zb_r[1, 3, r, cols]) + dec5(yb_r[r, cols])
            )

        hidden, gate_grad, up_grad = activate(total(0), total(FB), total(2 * FB))
        gb[row, r, 0:FB] = hidden
        gb[row, r, FB : 2 * FB] = gate_grad
        gb[row, r, 2 * FB : CB] = up_grad

    part = gb.at[row]
    sent.append(send(part, part, gby_ss, gby_rs, mate))
    gay_send(0)

    def products(at, off):
        piece = (z + off) % NZ
        both = pl.ds(2 * piece, 2)

        def part(ref, first, width):
            return ref[both, :, first : first + width].reshape(2 * T, width)

        outs = dot(part(ga, 0, FA), d_w[0:FA, :]) + dot(part(gb, 0, FB), d_w[FA:F, :])
        grads = (
            dot_t(part(ga, FA, FA), g_w[:, 0:FA])
            + dot_t(part(ga, 2 * FA, FA), u_w[:, 0:FA])
            + dot_t(part(gb, FB, FB), g_w[:, FA:F])
            + dot_t(part(gb, 2 * FB, FB), u_w[:, FA:F])
        )
        oi[at, :, :, 0:D] = outs.reshape(2, T, D)
        oi[at, :, :, D : 2 * D] = grads.reshape(2, T, D)
        send(oi.at[at, 1 - core], sib_r.at[at], sib_ss.at[at], sib_rs.at[at], sibling)

    def sib_copy(at):
        return pltpu.make_async_remote_copy(
            src_ref=oi.at[at, 1 - core], dst_ref=sib_r.at[at], send_sem=sib_ss.at[at], recv_sem=sib_rs.at[at],
            device_id=sibling, device_id_type=MESH,
        )

    def col_copy(at, side, dist, to):
        return pltpu.make_async_remote_copy(
            src_ref=col_s.at[at], dst_ref=col_r.at[side, dist - 1],
            send_sem=col_ss.at[side, dist - 1], recv_sem=col_rs.at[side, dist - 1],
            device_id=(row, to * 2 + core), device_id_type=MESH,
        )

    fin_move = pltpu.make_async_remote_copy(
        src_ref=fin_s, dst_ref=fin_r, send_sem=fin_ss, recv_sem=fin_rs,
        device_id=same_core(1), device_id_type=MESH,
    )

    def send_x(at, off):
        piece = (z + off) % NZ
        to_x, side = piece // 2, piece % 2
        sib_copy(at).wait_recv()

        @pl.when(to_x == x)
        def _():
            acc[side] = oi[at, core] + sib_r[at]

        @pl.when(to_x != x)
        def _():
            @rows(T)
            def _(r):
                col_s[at, r] = enc3(oi[at, core, r] + sib_r[at, r])

            col_copy(at, side, (to_x + 4 - x) % 4, to_x * 2 + yh).start()

    def reduce_x(off):
        piece = (z + off) % NZ
        side = piece % 2

        @pl.when(piece // 2 == x)
        def _():
            for dist in (1, 3, 2):
                col_copy(0, side, dist, chip).wait_recv()

            @rows(T)
            def _(r):
                total = acc[side, r] + dec3(col_r[side, 0, r]) + dec3(col_r[side, 1, r]) + dec3(col_r[side, 2, r])

                @pl.when(side == yh)
                def _():
                    out_ref[r] = total[:, 0:D]
                    ing_ref[r] = total[:, D : 2 * D]

                @pl.when(side != yh)
                def _():
                    fin_s[r] = enc3(total)

            @pl.when(side != yh)
            def _():
                fin_move.start()

    over = (((0,), (0,)), ((), ()))

    def wgrad_down():
        cots = xc[...].reshape(16 * T, D)
        for ref, width, first in ((ga, FA, 0), (gb, FB, FA)):
            hidden = ref[:, :, 0:width].reshape(16 * T, width)
            d_out[first : first + width, :] = lax.dot_general(hidden, cots, over, preferred_element_type=F32)

    def wgrad_in(out, third):
        for ref, width, first in ((ga, FA, 0), (gb, FB, FA)):
            grads = ref[:, :, third * width : (third + 1) * width].reshape(16 * T, width)
            out[:, first : first + width] = dot(ft[...], grads)

    gby = gb.at[mate[0]]
    pltpu.make_async_remote_copy(
        src_ref=gby, dst_ref=gby, send_sem=gby_ss, recv_sem=gby_rs, device_id=mate, device_id_type=MESH
    ).wait_recv()
    for way in range(2):
        gbz_send(way, 0)

    def offs_of(step):
        return (NZ - 1 - step, step + 1)

    for step in range(4):
        for way in range(2):
            gaz_wait(way, step)
            if step < 3:
                gaz_send(way, step + 1)
                gay_send(offs_of(step)[way])
        if step == 3:
            gay_send(4)
        if step == 0:
            gay_wait(0)
            products(0, 0)
        else:
            for way in range(2):
                off = offs_of(step - 1)[way]
                gay_wait(off)
                products(BPOS[off], off)
        for way in range(2):
            gbz_wait(way, step)
            if step < 3:
                gbz_send(way, step + 1)
        if step == 0:
            send_x(0, 0)
        else:
            for way in range(2):
                off = offs_of(step - 1)[way]
                send_x(BPOS[off], off)
            if step == 1:
                reduce_x(0)
            else:
                for way in range(2):
                    reduce_x(offs_of(step - 2)[way])

    gay_wait(4)
    products(7, 4)
    wgrad_down()
    send_x(7, 4)
    for way in range(2):
        reduce_x(offs_of(2)[way])
    wgrad_in(g_out, 1)
    reduce_x(4)
    wgrad_in(u_out, 2)
    fin_move.wait_recv()

    @rows(T)
    def _(r):
        out_ref[r] += dec3(fin_r[r, 0:D])
        ing_ref[r] += dec3(fin_r[r, D : 2 * D])

    for copy in sent:
        copy.wait_send()

    @pl.loop(0, NZ)
    def _(at):
        ya_copy(at, 0).wait_send()
        ya_copy(at, 1).wait_send()
        sib_copy(at).wait_send()

    for side in range(2):
        for dist in range(1, 4):
            col_copy(0, side, dist, chip).wait_send()
    fin_move.wait_send()


def layer(*operands):
    vmem = pltpu.VMEM
    dma = pltpu.SemaphoreType.DMA
    hbm = pl.BlockSpec(memory_space=pl.ANY)
    full = pl.BlockSpec(memory_space=pltpu.VMEM)
    return pl.pallas_call(
        layer_kernel,
        out_shape=(
            vmem((T, D), F32),
            vmem((T, D), F32),
            vmem((D, F), F32),
            vmem((D, F), F32),
            vmem((F, D), F32),
        ),
        in_specs=[hbm] * 5,
        out_specs=(full,) * 5,
        scratch_shapes=[
            vmem((D, F), BF16),
            vmem((D, F), BF16),
            vmem((F, D), BF16),
            vmem((16, T, D), BF16),
            vmem((16, T, D), BF16),
            vmem((D, 16 * T), BF16),
            vmem((NZ, 2 * T, CA), F32),
            vmem((NZ, 2 * T, CB), F32),
            vmem((NZ, T, CA), BF16),
            vmem((NZ, T, CA), BF16),
            vmem((T, CB), BF16),
            vmem((T, CB), BF16),
            vmem((2, 4, T, CA), BF16),
            vmem((2, 4, T, CA), BF16),
            vmem((2, 4, 2 * T, CB), BF16),
            vmem((2, 4, 2 * T, CB), BF16),
            vmem((16, T, CA), BF16),
            vmem((16, T, CB), BF16),
            vmem((NZ, 2, T, 2 * D), F32),
            vmem((NZ, T, 2 * D), F32),
            vmem((NZ, T, 2 * D), BF16),
            vmem((2, 3, T, 2 * D), BF16),
            vmem((2, T, 2 * D), F32),
            vmem((T, 2 * D), BF16),
            vmem((T, 2 * D), BF16),
            dma((5,)),
            dma((8,)), dma((8,)), dma((8,)), dma((8,)),
            dma((8,)), dma((8,)), dma((8,)), dma((8,)),
            dma((8, 2)), dma((8, 2)), dma, dma,
            dma((2, 4)), dma((2, 4)), dma((2, 4)), dma((2, 4)), dma((2,)), dma((2,)),
            dma((2, 4)), dma((2, 4)), dma((8,)), dma((8,)),
            dma((2, 4)), dma((2, 4)), dma, dma,
            dma((8,)), dma((8,)), dma((2, 3)), dma((2, 3)), dma, dma,
        ],
        compiler_params=pltpu.CompilerParams(
            collective_id=0, has_side_effects=True, vmem_limit_bytes=48 * 1024 * 1024
        ),
        name="layer",
    )(*[pltpu.with_memory_space_constraint(operand, pltpu.HBM) for operand in operands])


def store_kernel(*refs):
    sources, targets, sem = refs[:5], refs[5:10], refs[10]
    copies = []
    for n in (2, 3, 4, 0, 1):
        count = 4 if n >= 2 else 1
        size = sources[n].shape[0] // count
        for part in range(count):
            at = pl.ds(part * size, size)
            copies.append(pltpu.make_async_copy(sources[n].at[at], targets[n].at[at], sem.at[n, part]))
            copies[-1].start()
    for copy in copies:
        copy.wait()


def store(*arrays):
    return pl.pallas_call(
        store_kernel,
        out_shape=tuple(pltpu.HBM(array.shape, array.dtype) for array in arrays),
        in_specs=[pl.BlockSpec(memory_space=pltpu.VMEM)] * 5,
        out_specs=[pl.BlockSpec(memory_space=pl.ANY)] * 5,
        scratch_shapes=[pltpu.SemaphoreType.DMA((5, 4))],
        compiler_params=pltpu.CompilerParams(vmem_limit_bytes=4 * 1024 * 1024),
        name="store",
    )(*[pltpu.with_memory_space_constraint(array, pltpu.VMEM) for array in arrays])


def body(features, gate_weight, up_weight, down_weight, cotangent):
    return store(*layer(features, gate_weight, up_weight, down_weight, cotangent))


def solution(mesh):
    in_specs = (P("col", "row"), P("row", "col"), P("row", "col"), P("col", "row"), P("col", "row"))
    out_specs = (
        P("col", "row"),
        P("col", "row"),
        P("row", "col"),
        P("row", "col"),
        P("col", "row"),
    )
    return jax.shard_map(body, mesh=mesh, in_specs=in_specs, out_specs=out_specs, check_vma=False)
```

```python
import jax
import jax.numpy as jnp
from jax import lax
from jax.experimental import pallas as pl
from jax.experimental.pallas import tpu as pltpu
from jax.sharding import PartitionSpec as P

MESH = pl.DeviceIdType.MESH
F32, BF16 = jnp.float32, jnp.bfloat16
NZ = 8
T = 48
D = 512
FA, FB = 512, 384
F = FA + FB
CA, CB = 3 * FA, 3 * FB
HALF = CA // 2
SCALE = 4096.0
CSCALE = 1024.0
ORDER = (4, 3, 5, 2, 6, 1, 7, 0)
POS = {off: at for at, off in enumerate(ORDER)}
BACK = (0, 1, 7, 2, 6, 3, 5, 4)
BPOS = {off: at for at, off in enumerate(BACK)}


def enc5(value):
    value = value * SCALE
    square = value * value
    return (square * square * value).astype(BF16)


def dec5(code):
    code = code.astype(F32)
    root = jnp.exp2(jnp.log2(jnp.abs(code)) * 0.2) * (1.0 / SCALE)
    return jnp.where(code < 0, -root, root)


def enc3(value):
    value = value * CSCALE
    return (value * value * value).astype(BF16)


def dec3(code):
    code = code.astype(F32)
    root = jnp.exp2(jnp.log2(jnp.abs(code)) * (1.0 / 3.0)) * (1.0 / CSCALE)
    return jnp.where(code < 0, -root, root)


def dot(left, right):
    return jnp.dot(left, right, preferred_element_type=F32)


def dot_t(left, right):
    return lax.dot_general(left, right, (((1,), (1,)), ((), ())), preferred_element_type=F32)


def rows(count, step=16):
    def run(fn):
        @pl.loop(0, count // step)
        def _(i):
            fn(pl.ds(pl.multiple_of(i * step, step), step))

    return run


def layer_kernel(
    x_hbm, g_hbm, u_hbm, d_hbm, c_hbm,
    out_ref, ing_ref, g_out, u_out, d_out,
    g_w, u_w, d_w, xf, xc, ft, pa, pb, ya_s, ya_r, yb_s, yb_r, za_s, za_r, zb_s, zb_r,
    ga, gb, oi, sib_r, col_s, col_r, acc, fin_s, fin_r,
    load_sem, f_ss, f_rs, c_ss, c_rs, ff_ss, ff_rs, cf_ss, cf_rs, ya_ss, ya_rs, yb_ss, yb_rs,
    za_ss, za_rs, zb_ss, zb_rs, gaz_ss, gaz_rs, gay_ss, gay_rs, gbz_ss, gbz_rs, gby_ss, gby_rs,
    sib_ss, sib_rs, col_ss, col_rs, fin_ss, fin_rs,
):
    row, col = lax.axis_index("row"), lax.axis_index("col")
    z, yl = row // 2, row % 2
    chip, core = col // 2, col % 2
    x, yh = chip // 2, chip % 2

    def at_chip(k):
        return ((x + k // 2) % 4) * 2 + (yh + k % 2) % 2

    def from_chip(k):
        return ((x + 4 - k // 2) % 4) * 2 + (yh + k % 2) % 2

    def place(of_chip):
        return ((of_chip + 4 * core) % 8) * 2 + core

    up_z = ((z + 1) % NZ) * 2 + yl
    down_z = ((z + NZ - 1) % NZ) * 2 + yl
    mate = (z * 2 + 1 - yl, col)
    sibling = (row, chip * 2 + 1 - core)
    ring = ((up_z, col), (down_z, col))

    def send(src, dst, ss, rs, to):
        copy = pltpu.make_async_remote_copy(
            src_ref=src, dst_ref=dst, send_sem=ss, recv_sem=rs, device_id=to, device_id_type=MESH
        )
        copy.start()
        return copy

    sent = []

    loads = [
        pltpu.make_async_copy(x_hbm, xf.at[place(chip)], load_sem.at[0]),
        pltpu.make_async_copy(c_hbm, xc.at[place(chip)], load_sem.at[1]),
        pltpu.make_async_copy(g_hbm, g_w, load_sem.at[2]),
        pltpu.make_async_copy(u_hbm, u_w, load_sem.at[3]),
        pltpu.make_async_copy(d_hbm, d_w, load_sem.at[4]),
    ]
    for copy in loads:
        copy.start()

    barrier = pltpu.get_barrier_semaphore()
    for k in range(1, 8):
        pl.semaphore_signal(barrier, inc=1, device_id=(row, from_chip(k) * 2 + core), device_id_type=MESH)
    for to in (sibling, mate, ring[0], ring[1]):
        pl.semaphore_signal(barrier, inc=1, device_id=to, device_id_type=MESH)
    pl.semaphore_wait(barrier, 11)
    loads[0].wait()
    loads[1].wait()

    def arrival(ref, ss, rs):
        return pltpu.make_async_remote_copy(
            src_ref=ref, dst_ref=ref, send_sem=ss, recv_sem=rs, device_id=mate, device_id_type=MESH
        )

    def same_core(k):
        return (row, at_chip(k) * 2 + core)

    mine_f, mine_c = xf.at[place(chip)], xc.at[place(chip)]
    for k in (4, 5, 2, 6, 3, 7, 1):
        sent.append(send(mine_f, mine_f, f_ss.at[k], f_rs.at[k], same_core(k)))
    sent.append(send(mine_f, mine_f, ff_ss.at[0], ff_rs.at[0], sibling))
    for k in (1, 4, 2, 6):
        sent.append(send(mine_c, mine_c, c_ss.at[k], c_rs.at[k], same_core(k)))
    sent.append(send(mine_c, mine_c, cf_ss.at[0], cf_rs.at[0], sibling))

    def pass_on(ref, ss, rs, to_ss, to_rs, k):
        part = ref.at[place(from_chip(k))]
        arrival(part, ss.at[k], rs.at[k]).wait_recv()
        sent.append(send(part, part, to_ss.at[k], to_rs.at[k], sibling))

    for k in (1, 2, 6, 3, 7, 4, 5):
        pass_on(xf, f_ss, f_rs, ff_ss, ff_rs, k)
    pass_on(xc, c_ss, c_rs, cf_ss, cf_rs, 1)
    partner = xc.at[place(from_chip(1))]
    for k in (5, 3, 7):
        sent.append(send(partner, partner, c_ss.at[k], c_rs.at[k], same_core(k - 1)))
    for copy in loads[2:]:
        copy.wait()
    for k in range(8):
        arrival(mine_f, ff_ss.at[k], ff_rs.at[k]).wait_recv()

    def tokens(ref, off):
        piece = (z + off) % NZ
        return jnp.concatenate([ref[2 * piece + yl], ref[2 * piece + 1 - yl]], axis=0)

    def mates(r):
        return pl.ds(pl.multiple_of(r.start + T, 16), 16)

    def partial_gu(at, off):
        feats = tokens(xf, off)
        pa[at, :, 0:FA] = dot(feats, g_w[:, 0:FA])
        pa[at, :, FA : 2 * FA] = dot(feats, u_w[:, 0:FA])
        pb[at, :, 0:FB] = dot(feats, g_w[:, FA:F])
        pb[at, :, FB : 2 * FB] = dot(feats, u_w[:, FA:F])

        @rows(T)
        def _(r):
            ya_s[at, r, 0 : 2 * FA] = enc5(pa[at, mates(r), 0 : 2 * FA])

    def partial_h(at, off):
        cots = tokens(xc, off)
        pa[at, :, 2 * FA : CA] = dot_t(cots, d_w[0:FA, :])
        pb[at, :, 2 * FB : CB] = dot_t(cots, d_w[FA:F, :])

        @rows(T)
        def _(r):
            ya_s[at, r, 2 * FA : CA] = enc5(pa[at, mates(r), 2 * FA : CA])

    A_COLS = ((0, 2 * FA), (2 * FA, FA))
    B_COLS = ((0, 2 * FB), (2 * FB, FB))

    def ya_copy(at, which):
        cols = pl.ds(*A_COLS[which])
        return pltpu.make_async_remote_copy(
            src_ref=ya_s.at[at, :, cols], dst_ref=ya_r.at[at, :, cols],
            send_sem=ya_ss.at[at, which], recv_sem=ya_rs.at[at, which],
            device_id=mate, device_id_type=MESH,
        )

    def half(which, way):
        first, width = A_COLS[which]
        return pl.ds(first + way * (width // 2), width // 2)

    def za_copy(which, way, step):
        cols = pl.ds(*A_COLS[which]) if step else half(which, way)
        part = (way, step, slice(None), cols)
        return pltpu.make_async_remote_copy(
            src_ref=za_s.at[part], dst_ref=za_r.at[part],
            send_sem=za_ss.at[which, way, step], recv_sem=za_rs.at[which, way, step],
            device_id=ring[way], device_id_type=MESH,
        )

    def zb_copy(which, way, step):
        tok = slice(None) if step else pl.ds(way * T, T)
        part = (way, step, tok, pl.ds(*B_COLS[which]))
        return pltpu.make_async_remote_copy(
            src_ref=zb_s.at[part], dst_ref=zb_r.at[part],
            send_sem=zb_ss.at[which, way, step], recv_sem=zb_rs.at[which, way, step],
            device_id=ring[way], device_id_type=MESH,
        )

    def za_step(which, step):
        if step == 0:
            ya_copy(0, which).wait_recv()
        for way in range(2):
            at = POS[4 - step if way == 0 else 4 + step]
            if step:
                ya_copy(at, which).wait_recv()
                za_copy(which, way, step - 1).wait_recv()
            cols = pl.ds(*A_COLS[which])
            got, rest = half(which, way), half(which, 1 - way)

            @rows(T)
            def _(r):
                if step == 0:
                    za_s[way, 0, r, got] = enc5(pa[at, r, got] + dec5(ya_r[at, r, got]))
                elif step == 1:
                    za_s[way, 1, r, got] = enc5(
                        pa[at, r, got] + dec5(ya_r[at, r, got]) + dec5(za_r[way, 0, r, got])
                    )
                    za_s[way, 1, r, rest] = enc5(pa[at, r, rest] + dec5(ya_r[at, r, rest]))
                else:
                    za_s[way, step, r, cols] = enc5(
                        pa[at, r, cols] + dec5(ya_r[at, r, cols]) + dec5(za_r[way, step - 1, r, cols])
                    )

            copy = za_copy(which, way, step)
            copy.start()
            sent.append(copy)

    def zb_step(which, step):
        for way in range(2):
            at = POS[4 - step if way == 0 else 4 + step]
            if step:
                zb_copy(which, way, step - 1).wait_recv()
            cols = pl.ds(*B_COLS[which])

            def shifted(r, by):
                return pl.ds(pl.multiple_of(r.start + by, 16), 16)

            if step < 2:

                @rows(T)
                def _(r):
                    got, rest = shifted(r, way * T), shifted(r, (1 - way) * T)
                    if step == 0:
                        zb_s[way, 0, got, cols] = enc5(pb[at, got, cols])
                    else:
                        zb_s[way, 1, got, cols] = enc5(pb[at, got, cols] + dec5(zb_r[way, 0, got, cols]))
                        zb_s[way, 1, rest, cols] = enc5(pb[at, rest, cols])
            else:

                @rows(2 * T)
                def _(r):
                    zb_s[way, step, r, cols] = enc5(pb[at, r, cols] + dec5(zb_r[way, step - 1, r, cols]))

            copy = zb_copy(which, way, step)
            copy.start()
            sent.append(copy)

    def off_at(at):
        return jnp.where(at % 2 == 1, 4 - (at + 1) // 2, 4 + at // 2)

    partial_gu(0, 4)
    ya_copy(0, 0).start()
    zb_step(0, 0)

    @pl.loop(1, 3)
    def _(at):
        partial_gu(at, off_at(at))
        ya_copy(at, 0).start()

    @pl.loop(3, NZ)
    def _(at):
        partial_gu(at, off_at(at))

    zb_step(0, 1)
    for k in (2, 6, 4, 3, 7, 5):
        pass_on(xc, c_ss, c_rs, cf_ss, cf_rs, k)
    za_step(0, 0)
    for k in range(8):
        arrival(mine_c, cf_ss.at[k], cf_rs.at[k]).wait_recv()

    partial_h(0, 4)
    ya_copy(0, 1).start()
    zb_step(1, 0)

    @pl.loop(1, 3)
    def _(at):
        partial_h(at, off_at(at))
        ya_copy(at, 1).start()

    @pl.loop(3, NZ)
    def _(at):
        partial_h(at, off_at(at))
        ya_copy(at, 0).start()
        ya_copy(at, 1).start()

    zb_step(0, 2)
    za_step(0, 1)
    zb_step(1, 1)
    za_step(1, 0)
    zb_step(0, 3)
    zb_step(1, 2)
    za_step(1, 1)
    zb_step(1, 3)
    ft[...] = xf[...].reshape(16 * T, D).T
    za_step(0, 2)
    za_step(1, 2)

    for which in range(2):
        for way in range(2):
            zb_copy(which, way, 3).wait_recv()

    @rows(T)
    def _(r):
        r2 = pl.ds(pl.multiple_of(r.start + T, 16), 16)
        yb_s[r] = enc5(pb[7, r2] + dec5(zb_r[0, 3, r2]) + dec5(zb_r[1, 3, r2]))

    yb_move = send(yb_s, yb_r, yb_ss, yb_rs, mate)
    sent.append(yb_move)

    def activate(gate, up, hid):
        sig = jax.nn.sigmoid(gate)
        silu = gate * sig
        return (
            (silu * up).astype(BF16),
            (hid * up * sig * (1.0 + gate * (1.0 - sig))).astype(BF16),
            (hid * silu).astype(BF16),
        )

    za_step(0, 3)
    za_step(1, 3)
    for which in range(2):
        ya_copy(7, which).wait_recv()
        for way in range(2):
            za_copy(which, way, 3).wait_recv()

    @rows(T)
    def _(r):
        def total(first):
            cols = pl.ds(first, FA)
            return pa[7, r, cols] + dec5(ya_r[7, r, cols]) + dec5(za_r[0, 3, r, cols]) + dec5(za_r[1, 3, r, cols])

        hidden, gate_grad, up_grad = activate(total(0), total(FA), total(2 * FA))
        ga[row, r, 0:FA] = hidden
        ga[row, r, FA : 2 * FA] = gate_grad
        ga[row, r, 2 * FA : CA] = up_grad

    def gaz_send(way, step):
        src = ((z + NZ - step) % NZ if way == 0 else (z + step) % NZ) * 2 + yl
        if step < 3:
            part = ga.at[src]
        else:
            part = ga.at[src, :, pl.ds(way * HALF, HALF)]
        copy = send(part, part, gaz_ss.at[way, step], gaz_rs.at[way, step], ring[way])
        sent.append(copy)

    def gaz_wait(way, step):
        src = ((z + NZ - 1 - step) % NZ if way == 0 else (z + step + 1) % NZ) * 2 + yl
        if step < 3:
            part = ga.at[src]
        else:
            part = ga.at[src, :, pl.ds(way * HALF, HALF)]
        pltpu.make_async_remote_copy(
            src_ref=part, dst_ref=part, send_sem=gaz_ss.at[way, step], recv_sem=gaz_rs.at[way, step],
            device_id=mate, device_id_type=MESH,
        ).wait_recv()

    def gay_send(off):
        part = ga.at[((z + off) % NZ) * 2 + yl]
        sent.append(send(part, part, gay_ss.at[off], gay_rs.at[off], mate))

    def gay_wait(off):
        part = ga.at[((z + off) % NZ) * 2 + 1 - yl]
        pltpu.make_async_remote_copy(
            src_ref=part, dst_ref=part, send_sem=gay_ss.at[off], recv_sem=gay_rs.at[off],
            device_id=mate, device_id_type=MESH,
        ).wait_recv()

    def gbz_part(way, step, src):
        if step < 3:
            return gb.at[pl.ds(2 * src, 2)]
        return gb.at[2 * src + way]

    def gbz_send(way, step):
        part = gbz_part(way, step, (z + NZ - step) % NZ if way == 0 else (z + step) % NZ)
        sent.append(send(part, part, gbz_ss.at[way, step], gbz_rs.at[way, step], ring[way]))

    def gbz_wait(way, step):
        part = gbz_part(way, step, (z + NZ - 1 - step) % NZ if way == 0 else (z + step + 1) % NZ)
        pltpu.make_async_remote_copy(
            src_ref=part, dst_ref=part, send_sem=gbz_ss.at[way, step], recv_sem=gbz_rs.at[way, step],
            device_id=mate, device_id_type=MESH,
        ).wait_recv()

    for way in range(2):
        gaz_send(way, 0)
    yb_move.wait_recv()

    @rows(T)
    def _(r):
        def total(first):
            cols = pl.ds(first, FB)
            return (
                pb[7, r, cols] + dec5(zb_r[0, 3, r, cols]) + dec5(zb_r[1, 3, r, cols]) + dec5(yb_r[r, cols])
            )

        hidden, gate_grad, up_grad = activate(total(0), total(FB), total(2 * FB))
        gb[row, r, 0:FB] = hidden
        gb[row, r, FB : 2 * FB] = gate_grad
        gb[row, r, 2 * FB : CB] = up_grad

    part = gb.at[row]
    sent.append(send(part, part, gby_ss, gby_rs, mate))
    gay_send(0)

    def products(at, off):
        piece = (z + off) % NZ
        both = pl.ds(2 * piece, 2)

        def part(ref, first, width):
            return ref[both, :, first : first + width].reshape(2 * T, width)

        outs = dot(part(ga, 0, FA), d_w[0:FA, :]) + dot(part(gb, 0, FB), d_w[FA:F, :])
        oi[at, :, :, 0:D] = outs.reshape(2, T, D)
        sib_copy(at, 0).start()
        grads = (
            dot_t(part(ga, FA, FA), g_w[:, 0:FA])
            + dot_t(part(ga, 2 * FA, FA), u_w[:, 0:FA])
            + dot_t(part(gb, FB, FB), g_w[:, FA:F])
            + dot_t(part(gb, 2 * FB, FB), u_w[:, FA:F])
        )
        oi[at, :, :, D : 2 * D] = grads.reshape(2, T, D)
        sib_copy(at, 1).start()

    OUTS = (pl.ds(0, D), pl.ds(D, D))

    def sib_copy(at, which):
        cols = OUTS[which]
        return pltpu.make_async_remote_copy(
            src_ref=oi.at[at, 1 - core, :, cols], dst_ref=sib_r.at[at, :, cols],
            send_sem=sib_ss.at[at, which], recv_sem=sib_rs.at[at, which],
            device_id=sibling, device_id_type=MESH,
        )

    def col_copy(at, side, dist, to, which):
        cols = OUTS[which]
        return pltpu.make_async_remote_copy(
            src_ref=col_s.at[at, :, cols], dst_ref=col_r.at[side, dist - 1, :, cols],
            send_sem=col_ss.at[side, dist - 1, which], recv_sem=col_rs.at[side, dist - 1, which],
            device_id=(row, to * 2 + core), device_id_type=MESH,
        )

    def fin_copy(which):
        cols = OUTS[which]
        return pltpu.make_async_remote_copy(
            src_ref=fin_s.at[:, cols], dst_ref=fin_r.at[:, cols], send_sem=fin_ss.at[which],
            recv_sem=fin_rs.at[which], device_id=same_core(1), device_id_type=MESH,
        )

    def send_x(at, off):
        owner = (z + off + 4 * core) % NZ
        to_x, side = owner // 2, owner % 2
        for which in range(2):
            cols = OUTS[which]
            sib_copy(at, which).wait_recv()

            @pl.when(to_x == x)
            def _():
                acc[side, :, cols] = oi[at, core, :, cols] + sib_r[at, :, cols]

            @pl.when(to_x != x)
            def _():
                @rows(T)
                def _(r):
                    col_s[at, r, cols] = enc3(oi[at, core, r, cols] + sib_r[at, r, cols])

                col_copy(at, side, (to_x + 4 - x) % 4, to_x * 2 + yh, which).start()

    def reduce_x(off):
        owner = (z + off + 4 * core) % NZ
        side = owner % 2

        @pl.when(owner // 2 == x)
        def _():
            for which in range(2):
                cols = OUTS[which]
                for dist in (1, 3, 2):
                    col_copy(0, side, dist, chip, which).wait_recv()

                @rows(T)
                def _(r):
                    total = (
                        acc[side, r, cols] + dec3(col_r[side, 0, r, cols])
                        + dec3(col_r[side, 1, r, cols]) + dec3(col_r[side, 2, r, cols])
                    )

                    @pl.when(side == yh)
                    def _():
                        (out_ref, ing_ref)[which][r] = total

                    @pl.when(side != yh)
                    def _():
                        fin_s[r, cols] = enc3(total)

                @pl.when(side != yh)
                def _():
                    fin_copy(which).start()

    over = (((0,), (0,)), ((), ()))

    def wgrad_down():
        cots = xc[...].reshape(16 * T, D)
        for ref, width, first in ((ga, FA, 0), (gb, FB, FA)):
            hidden = ref[:, :, 0:width].reshape(16 * T, width)
            d_out[first : first + width, :] = lax.dot_general(hidden, cots, over, preferred_element_type=F32)

    def wgrad_in(out, third):
        for ref, width, first in ((ga, FA, 0), (gb, FB, FA)):
            grads = ref[:, :, third * width : (third + 1) * width].reshape(16 * T, width)
            out[:, first : first + width] = dot(ft[...], grads)

    gby = gb.at[mate[0]]
    pltpu.make_async_remote_copy(
        src_ref=gby, dst_ref=gby, send_sem=gby_ss, recv_sem=gby_rs, device_id=mate, device_id_type=MESH
    ).wait_recv()
    for way in range(2):
        gbz_send(way, 0)

    def offs_of(step):
        return (NZ - 1 - step, step + 1)

    for step in range(4):
        for way in range(2):
            gaz_wait(way, step)
            if step < 3:
                gaz_send(way, step + 1)
                gay_send(offs_of(step)[way])
        if step == 3:
            gay_send(4)
        if step == 0:
            gay_wait(0)
            products(0, 0)
        else:
            for way in range(2):
                off = offs_of(step - 1)[way]
                gay_wait(off)
                products(BPOS[off], off)
        if step == 3:
            for way in range(2):
                off = offs_of(2)[way]
                send_x(BPOS[off], off)
            for way in range(2):
                reduce_x(offs_of(1)[way])
        for way in range(2):
            gbz_wait(way, step)
            if step < 3:
                gbz_send(way, step + 1)
        if step == 0:
            send_x(0, 0)
        elif step < 3:
            for way in range(2):
                off = offs_of(step - 1)[way]
                send_x(BPOS[off], off)
            if step == 1:
                reduce_x(0)
            else:
                for way in range(2):
                    reduce_x(offs_of(step - 2)[way])

    gay_wait(4)
    products(7, 4)
    send_x(7, 4)
    for way in range(2):
        reduce_x(offs_of(2)[way])
    wgrad_down()
    wgrad_in(g_out, 1)
    reduce_x(4)
    wgrad_in(u_out, 2)
    for which in range(2):
        fin_copy(which).wait_recv()

        @rows(T)
        def _(r):
            (out_ref, ing_ref)[which][r] += dec3(fin_r[r, OUTS[which]])

    for copy in sent:
        copy.wait_send()

    @pl.loop(0, NZ)
    def _(at):
        ya_copy(at, 0).wait_send()
        ya_copy(at, 1).wait_send()
        sib_copy(at, 0).wait_send()
        sib_copy(at, 1).wait_send()

    for side in range(2):
        for dist in range(1, 4):
            for which in range(2):
                col_copy(0, side, dist, chip, which).wait_send()
    fin_copy(0).wait_send()
    fin_copy(1).wait_send()


def layer(*operands):
    vmem = pltpu.VMEM
    dma = pltpu.SemaphoreType.DMA
    hbm = pl.BlockSpec(memory_space=pl.ANY)
    full = pl.BlockSpec(memory_space=pltpu.VMEM)
    return pl.pallas_call(
        layer_kernel,
        out_shape=(
            vmem((T, D), F32),
            vmem((T, D), F32),
            vmem((D, F), F32),
            vmem((D, F), F32),
            vmem((F, D), F32),
        ),
        in_specs=[hbm] * 5,
        out_specs=(full,) * 5,
        scratch_shapes=[
            vmem((D, F), BF16),
            vmem((D, F), BF16),
            vmem((F, D), BF16),
            vmem((16, T, D), BF16),
            vmem((16, T, D), BF16),
            vmem((D, 16 * T), BF16),
            vmem((NZ, 2 * T, CA), F32),
            vmem((NZ, 2 * T, CB), F32),
            vmem((NZ, T, CA), BF16),
            vmem((NZ, T, CA), BF16),
            vmem((T, CB), BF16),
            vmem((T, CB), BF16),
            vmem((2, 4, T, CA), BF16),
            vmem((2, 4, T, CA), BF16),
            vmem((2, 4, 2 * T, CB), BF16),
            vmem((2, 4, 2 * T, CB), BF16),
            vmem((16, T, CA), BF16),
            vmem((16, T, CB), BF16),
            vmem((NZ, 2, T, 2 * D), F32),
            vmem((NZ, T, 2 * D), F32),
            vmem((NZ, T, 2 * D), BF16),
            vmem((2, 3, T, 2 * D), BF16),
            vmem((2, T, 2 * D), F32),
            vmem((T, 2 * D), BF16),
            vmem((T, 2 * D), BF16),
            dma((5,)),
            dma((8,)), dma((8,)), dma((8,)), dma((8,)),
            dma((8,)), dma((8,)), dma((8,)), dma((8,)),
            dma((8, 2)), dma((8, 2)), dma, dma,
            dma((2, 2, 4)), dma((2, 2, 4)), dma((2, 2, 4)), dma((2, 2, 4)),
            dma((2, 4)), dma((2, 4)), dma((8,)), dma((8,)),
            dma((2, 4)), dma((2, 4)), dma, dma,
            dma((8, 2)), dma((8, 2)), dma((2, 3, 2)), dma((2, 3, 2)), dma((2,)), dma((2,)),
        ],
        compiler_params=pltpu.CompilerParams(
            collective_id=0, has_side_effects=True, vmem_limit_bytes=48 * 1024 * 1024
        ),
        name="layer",
    )(*[pltpu.with_memory_space_constraint(operand, pltpu.HBM) for operand in operands])


def store_kernel(*refs):
    sources, targets, sem = refs[:5], refs[5:10], refs[10]
    copies = []
    for n in (2, 3, 4, 0, 1):
        count = 4 if n >= 2 else 1
        size = sources[n].shape[0] // count
        for part in range(count):
            at = pl.ds(part * size, size)
            copies.append(pltpu.make_async_copy(sources[n].at[at], targets[n].at[at], sem.at[n, part]))
            copies[-1].start()
    for copy in copies:
        copy.wait()


def store(*arrays):
    return pl.pallas_call(
        store_kernel,
        out_shape=tuple(pltpu.HBM(array.shape, array.dtype) for array in arrays),
        in_specs=[pl.BlockSpec(memory_space=pltpu.VMEM)] * 5,
        out_specs=[pl.BlockSpec(memory_space=pl.ANY)] * 5,
        scratch_shapes=[pltpu.SemaphoreType.DMA((5, 4))],
        compiler_params=pltpu.CompilerParams(vmem_limit_bytes=4 * 1024 * 1024),
        name="store",
    )(*[pltpu.with_memory_space_constraint(array, pltpu.VMEM) for array in arrays])


def body(features, gate_weight, up_weight, down_weight, cotangent):
    return store(*layer(features, gate_weight, up_weight, down_weight, cotangent))


def solution(mesh):
    in_specs = (P("col", "row"), P("row", "col"), P("row", "col"), P("col", "row"), P("col", "row"))
    out_specs = (
        P("col", "row"),
        P("col", "row"),
        P("row", "col"),
        P("row", "col"),
        P("col", "row"),
    )
    return jax.shard_map(body, mesh=mesh, in_specs=in_specs, out_specs=out_specs, check_vma=False)
```

```python
import jax
import jax.numpy as jnp
from jax import lax
from jax.experimental import pallas as pl
from jax.experimental.pallas import tpu as pltpu
from jax.sharding import PartitionSpec as P

MESH = pl.DeviceIdType.MESH
F32, BF16 = jnp.float32, jnp.bfloat16
NZ = 8
T = 48
D = 512
FA, FB = 512, 384
F = FA + FB
CA, CB = 3 * FA, 3 * FB
HALF = CA // 2
SCALE = 4096.0
CSCALE = 1024.0
ORDER = (4, 3, 5, 2, 6, 1, 7, 0)
POS = {off: at for at, off in enumerate(ORDER)}
BACK = (0, 1, 7, 2, 6, 3, 5, 4)
BPOS = {off: at for at, off in enumerate(BACK)}


def enc5(value):
    value = value * SCALE
    square = value * value
    return (square * square * value).astype(BF16)


def dec5(code):
    code = code.astype(F32)
    root = jnp.exp2(jnp.log2(jnp.abs(code)) * 0.2) * (1.0 / SCALE)
    return jnp.where(code < 0, -root, root)


def enc3(value):
    value = value * CSCALE
    return (value * value * value).astype(BF16)


def dec3(code):
    code = code.astype(F32)
    root = jnp.exp2(jnp.log2(jnp.abs(code)) * (1.0 / 3.0)) * (1.0 / CSCALE)
    return jnp.where(code < 0, -root, root)


def dot(left, right):
    return jnp.dot(left, right, preferred_element_type=F32)


def dot_t(left, right):
    return lax.dot_general(left, right, (((1,), (1,)), ((), ())), preferred_element_type=F32)


def rows(count, step=16):
    def run(fn):
        @pl.loop(0, count // step)
        def _(i):
            fn(pl.ds(pl.multiple_of(i * step, step), step))

    return run


def layer_kernel(
    x_hbm, g_hbm, u_hbm, d_hbm, c_hbm,
    out_ref, ing_ref, g_out, u_out, d_out,
    g_w, u_w, d_w, xf, xc, ft, pa, pb, ya_s, ya_r, yb_s, yb_r, za_s, za_r, zb_s, zb_r,
    ga, gb, oi, sib_r, col_s, col_r, acc, fin_s, fin_r, last_r,
    load_sem, f_ss, f_rs, c_ss, c_rs, ff_ss, ff_rs, cf_ss, cf_rs, ya_ss, ya_rs, yb_ss, yb_rs,
    za_ss, za_rs, zb_ss, zb_rs, gaz_ss, gaz_rs, gay_ss, gay_rs, gbz_ss, gbz_rs, gby_ss, gby_rs,
    sib_ss, sib_rs, col_ss, col_rs, fin_ss, fin_rs, last_ss, last_rs,
):
    row, col = lax.axis_index("row"), lax.axis_index("col")
    z, yl = row // 2, row % 2
    chip, core = col // 2, col % 2
    x, yh = chip // 2, chip % 2

    def at_chip(k):
        return ((x + k // 2) % 4) * 2 + (yh + k % 2) % 2

    def from_chip(k):
        return ((x + 4 - k // 2) % 4) * 2 + (yh + k % 2) % 2

    def place(of_chip):
        return ((of_chip + 4 * core) % 8) * 2 + core

    up_z = ((z + 1) % NZ) * 2 + yl
    down_z = ((z + NZ - 1) % NZ) * 2 + yl
    mate = (z * 2 + 1 - yl, col)
    sibling = (row, chip * 2 + 1 - core)
    ring = ((up_z, col), (down_z, col))

    def send(src, dst, ss, rs, to):
        copy = pltpu.make_async_remote_copy(
            src_ref=src, dst_ref=dst, send_sem=ss, recv_sem=rs, device_id=to, device_id_type=MESH
        )
        copy.start()
        return copy

    sent = []

    loads = [
        pltpu.make_async_copy(x_hbm, xf.at[place(chip)], load_sem.at[0]),
        pltpu.make_async_copy(c_hbm, xc.at[place(chip)], load_sem.at[1]),
        pltpu.make_async_copy(g_hbm, g_w, load_sem.at[2]),
        pltpu.make_async_copy(u_hbm, u_w, load_sem.at[3]),
        pltpu.make_async_copy(d_hbm, d_w, load_sem.at[4]),
    ]
    for copy in loads:
        copy.start()

    barrier = pltpu.get_barrier_semaphore()
    for k in range(1, 8):
        pl.semaphore_signal(barrier, inc=1, device_id=(row, from_chip(k) * 2 + core), device_id_type=MESH)
    for to in (sibling, mate, ring[0], ring[1]):
        pl.semaphore_signal(barrier, inc=1, device_id=to, device_id_type=MESH)
    pl.semaphore_wait(barrier, 11)
    loads[0].wait()
    loads[1].wait()

    def arrival(ref, ss, rs):
        return pltpu.make_async_remote_copy(
            src_ref=ref, dst_ref=ref, send_sem=ss, recv_sem=rs, device_id=mate, device_id_type=MESH
        )

    def same_core(k):
        return (row, at_chip(k) * 2 + core)

    mine_f, mine_c = xf.at[place(chip)], xc.at[place(chip)]
    for k in (4, 5, 2, 6, 3, 7, 1):
        sent.append(send(mine_f, mine_f, f_ss.at[k], f_rs.at[k], same_core(k)))
    sent.append(send(mine_f, mine_f, ff_ss.at[0], ff_rs.at[0], sibling))
    for k in (1, 4, 2, 6):
        sent.append(send(mine_c, mine_c, c_ss.at[k], c_rs.at[k], same_core(k)))
    sent.append(send(mine_c, mine_c, cf_ss.at[0], cf_rs.at[0], sibling))

    def pass_on(ref, ss, rs, to_ss, to_rs, k):
        part = ref.at[place(from_chip(k))]
        arrival(part, ss.at[k], rs.at[k]).wait_recv()
        sent.append(send(part, part, to_ss.at[k], to_rs.at[k], sibling))

    for k in (1, 2, 6, 3, 7, 4, 5):
        pass_on(xf, f_ss, f_rs, ff_ss, ff_rs, k)
    pass_on(xc, c_ss, c_rs, cf_ss, cf_rs, 1)
    partner = xc.at[place(from_chip(1))]
    for k in (5, 3, 7):
        sent.append(send(partner, partner, c_ss.at[k], c_rs.at[k], same_core(k - 1)))
    for copy in loads[2:]:
        copy.wait()
    for k in range(8):
        arrival(mine_f, ff_ss.at[k], ff_rs.at[k]).wait_recv()

    def tokens(ref, off):
        piece = (z + off) % NZ
        return jnp.concatenate([ref[2 * piece + yl], ref[2 * piece + 1 - yl]], axis=0)

    def mates(r):
        return pl.ds(pl.multiple_of(r.start + T, 16), 16)

    def partial_gu(at, off):
        feats = tokens(xf, off)
        pa[at, :, 0:FA] = dot(feats, g_w[:, 0:FA])
        pa[at, :, FA : 2 * FA] = dot(feats, u_w[:, 0:FA])
        pb[at, :, 0:FB] = dot(feats, g_w[:, FA:F])
        pb[at, :, FB : 2 * FB] = dot(feats, u_w[:, FA:F])

        @rows(T)
        def _(r):
            ya_s[at, r, 0 : 2 * FA] = enc5(pa[at, mates(r), 0 : 2 * FA])

    def partial_h(at, off):
        cots = tokens(xc, off)
        pa[at, :, 2 * FA : CA] = dot_t(cots, d_w[0:FA, :])
        pb[at, :, 2 * FB : CB] = dot_t(cots, d_w[FA:F, :])

        @rows(T)
        def _(r):
            ya_s[at, r, 2 * FA : CA] = enc5(pa[at, mates(r), 2 * FA : CA])

    A_COLS = ((0, 2 * FA), (2 * FA, FA))
    B_COLS = ((0, 2 * FB), (2 * FB, FB))

    def ya_copy(at, which):
        cols = pl.ds(*A_COLS[which])
        return pltpu.make_async_remote_copy(
            src_ref=ya_s.at[at, :, cols], dst_ref=ya_r.at[at, :, cols],
            send_sem=ya_ss.at[at, which], recv_sem=ya_rs.at[at, which],
            device_id=mate, device_id_type=MESH,
        )

    def half(which, way):
        first, width = A_COLS[which]
        return pl.ds(first + way * (width // 2), width // 2)

    def za_copy(which, way, step):
        cols = pl.ds(*A_COLS[which]) if step else half(which, way)
        part = (way, step, slice(None), cols)
        return pltpu.make_async_remote_copy(
            src_ref=za_s.at[part], dst_ref=za_r.at[part],
            send_sem=za_ss.at[which, way, step], recv_sem=za_rs.at[which, way, step],
            device_id=ring[way], device_id_type=MESH,
        )

    def zb_copy(which, way, step):
        tok = slice(None) if step else pl.ds(way * T, T)
        part = (way, step, tok, pl.ds(*B_COLS[which]))
        return pltpu.make_async_remote_copy(
            src_ref=zb_s.at[part], dst_ref=zb_r.at[part],
            send_sem=zb_ss.at[which, way, step], recv_sem=zb_rs.at[which, way, step],
            device_id=ring[way], device_id_type=MESH,
        )

    def za_step(which, step):
        if step == 0:
            ya_copy(0, which).wait_recv()
        for way in range(2):
            at = POS[4 - step if way == 0 else 4 + step]
            if step:
                ya_copy(at, which).wait_recv()
                za_copy(which, way, step - 1).wait_recv()
            cols = pl.ds(*A_COLS[which])
            got, rest = half(which, way), half(which, 1 - way)

            @rows(T)
            def _(r):
                if step == 0:
                    za_s[way, 0, r, got] = enc5(pa[at, r, got] + dec5(ya_r[at, r, got]))
                elif step == 1:
                    za_s[way, 1, r, got] = enc5(
                        pa[at, r, got] + dec5(ya_r[at, r, got]) + dec5(za_r[way, 0, r, got])
                    )
                    za_s[way, 1, r, rest] = enc5(pa[at, r, rest] + dec5(ya_r[at, r, rest]))
                else:
                    za_s[way, step, r, cols] = enc5(
                        pa[at, r, cols] + dec5(ya_r[at, r, cols]) + dec5(za_r[way, step - 1, r, cols])
                    )

            copy = za_copy(which, way, step)
            copy.start()
            sent.append(copy)

    def zb_step(which, step):
        for way in range(2):
            at = POS[4 - step if way == 0 else 4 + step]
            if step:
                zb_copy(which, way, step - 1).wait_recv()
            cols = pl.ds(*B_COLS[which])

            def shifted(r, by):
                return pl.ds(pl.multiple_of(r.start + by, 16), 16)

            if step < 2:

                @rows(T)
                def _(r):
                    got, rest = shifted(r, way * T), shifted(r, (1 - way) * T)
                    if step == 0:
                        zb_s[way, 0, got, cols] = enc5(pb[at, got, cols])
                    else:
                        zb_s[way, 1, got, cols] = enc5(pb[at, got, cols] + dec5(zb_r[way, 0, got, cols]))
                        zb_s[way, 1, rest, cols] = enc5(pb[at, rest, cols])
            else:

                @rows(2 * T)
                def _(r):
                    zb_s[way, step, r, cols] = enc5(pb[at, r, cols] + dec5(zb_r[way, step - 1, r, cols]))

            copy = zb_copy(which, way, step)
            copy.start()
            sent.append(copy)

    def off_at(at):
        return jnp.where(at % 2 == 1, 4 - (at + 1) // 2, 4 + at // 2)

    partial_gu(0, 4)
    ya_copy(0, 0).start()
    zb_step(0, 0)

    @pl.loop(1, 3)
    def _(at):
        partial_gu(at, off_at(at))
        ya_copy(at, 0).start()

    @pl.loop(3, NZ)
    def _(at):
        partial_gu(at, off_at(at))

    zb_step(0, 1)
    for k in (2, 6, 4, 3, 7, 5):
        pass_on(xc, c_ss, c_rs, cf_ss, cf_rs, k)
    za_step(0, 0)
    for k in range(8):
        arrival(mine_c, cf_ss.at[k], cf_rs.at[k]).wait_recv()

    partial_h(0, 4)
    ya_copy(0, 1).start()
    zb_step(1, 0)

    @pl.loop(1, 3)
    def _(at):
        partial_h(at, off_at(at))
        ya_copy(at, 1).start()

    @pl.loop(3, NZ)
    def _(at):
        partial_h(at, off_at(at))
        ya_copy(at, 0).start()
        ya_copy(at, 1).start()

    zb_step(0, 2)
    za_step(0, 1)
    zb_step(1, 1)
    za_step(1, 0)
    zb_step(0, 3)
    zb_step(1, 2)
    za_step(1, 1)
    zb_step(1, 3)
    ft[...] = xf[...].reshape(16 * T, D).T
    za_step(0, 2)
    za_step(1, 2)

    for which in range(2):
        for way in range(2):
            zb_copy(which, way, 3).wait_recv()

    @rows(T)
    def _(r):
        r2 = pl.ds(pl.multiple_of(r.start + T, 16), 16)
        yb_s[r] = enc5(pb[7, r2] + dec5(zb_r[0, 3, r2]) + dec5(zb_r[1, 3, r2]))

    yb_move = send(yb_s, yb_r, yb_ss, yb_rs, mate)
    sent.append(yb_move)

    def activate(gate, up, hid):
        sig = jax.nn.sigmoid(gate)
        silu = gate * sig
        return (
            (silu * up).astype(BF16),
            (hid * up * sig * (1.0 + gate * (1.0 - sig))).astype(BF16),
            (hid * silu).astype(BF16),
        )

    za_step(0, 3)
    za_step(1, 3)
    for which in range(2):
        ya_copy(7, which).wait_recv()
        for way in range(2):
            za_copy(which, way, 3).wait_recv()

    @rows(T)
    def _(r):
        def total(first):
            cols = pl.ds(first, FA)
            return pa[7, r, cols] + dec5(ya_r[7, r, cols]) + dec5(za_r[0, 3, r, cols]) + dec5(za_r[1, 3, r, cols])

        hidden, gate_grad, up_grad = activate(total(0), total(FA), total(2 * FA))
        ga[row, r, 0:FA] = hidden
        ga[row, r, FA : 2 * FA] = gate_grad
        ga[row, r, 2 * FA : CA] = up_grad

    def gaz_send(way, step):
        src = ((z + NZ - step) % NZ if way == 0 else (z + step) % NZ) * 2 + yl
        if step < 3:
            part = ga.at[src]
        else:
            part = ga.at[src, :, pl.ds(way * HALF, HALF)]
        copy = send(part, part, gaz_ss.at[way, step], gaz_rs.at[way, step], ring[way])
        sent.append(copy)

    def gaz_wait(way, step):
        src = ((z + NZ - 1 - step) % NZ if way == 0 else (z + step + 1) % NZ) * 2 + yl
        if step < 3:
            part = ga.at[src]
        else:
            part = ga.at[src, :, pl.ds(way * HALF, HALF)]
        pltpu.make_async_remote_copy(
            src_ref=part, dst_ref=part, send_sem=gaz_ss.at[way, step], recv_sem=gaz_rs.at[way, step],
            device_id=mate, device_id_type=MESH,
        ).wait_recv()

    def gay_send(off):
        part = ga.at[((z + off) % NZ) * 2 + yl]
        sent.append(send(part, part, gay_ss.at[off], gay_rs.at[off], mate))

    def gay_wait(off):
        part = ga.at[((z + off) % NZ) * 2 + 1 - yl]
        pltpu.make_async_remote_copy(
            src_ref=part, dst_ref=part, send_sem=gay_ss.at[off], recv_sem=gay_rs.at[off],
            device_id=mate, device_id_type=MESH,
        ).wait_recv()

    def gbz_part(way, step, src):
        if step < 3:
            return gb.at[pl.ds(2 * src, 2)]
        return gb.at[2 * src + way]

    def gbz_send(way, step):
        part = gbz_part(way, step, (z + NZ - step) % NZ if way == 0 else (z + step) % NZ)
        sent.append(send(part, part, gbz_ss.at[way, step], gbz_rs.at[way, step], ring[way]))

    def gbz_wait(way, step):
        part = gbz_part(way, step, (z + NZ - 1 - step) % NZ if way == 0 else (z + step + 1) % NZ)
        pltpu.make_async_remote_copy(
            src_ref=part, dst_ref=part, send_sem=gbz_ss.at[way, step], recv_sem=gbz_rs.at[way, step],
            device_id=mate, device_id_type=MESH,
        ).wait_recv()

    for way in range(2):
        gaz_send(way, 0)
    yb_move.wait_recv()

    @rows(T)
    def _(r):
        def total(first):
            cols = pl.ds(first, FB)
            return (
                pb[7, r, cols] + dec5(zb_r[0, 3, r, cols]) + dec5(zb_r[1, 3, r, cols]) + dec5(yb_r[r, cols])
            )

        hidden, gate_grad, up_grad = activate(total(0), total(FB), total(2 * FB))
        gb[row, r, 0:FB] = hidden
        gb[row, r, FB : 2 * FB] = gate_grad
        gb[row, r, 2 * FB : CB] = up_grad

    part = gb.at[row]
    sent.append(send(part, part, gby_ss, gby_rs, mate))
    gay_send(0)

    def products(at, off):
        piece = (z + off) % NZ
        both = pl.ds(2 * piece, 2)

        def part(ref, first, width):
            return ref[both, :, first : first + width].reshape(2 * T, width)

        outs = dot(part(ga, 0, FA), d_w[0:FA, :]) + dot(part(gb, 0, FB), d_w[FA:F, :])
        oi[at, :, :, 0:D] = outs.reshape(2, T, D)
        sib_copy(at, 0).start()
        grads = (
            dot_t(part(ga, FA, FA), g_w[:, 0:FA])
            + dot_t(part(ga, 2 * FA, FA), u_w[:, 0:FA])
            + dot_t(part(gb, FB, FB), g_w[:, FA:F])
            + dot_t(part(gb, 2 * FB, FB), u_w[:, FA:F])
        )
        oi[at, :, :, D : 2 * D] = grads.reshape(2, T, D)
        sib_copy(at, 1).start()

    OUTS = (pl.ds(0, D), pl.ds(D, D))

    def sib_copy(at, which):
        cols = OUTS[which]
        return pltpu.make_async_remote_copy(
            src_ref=oi.at[at, 1 - core, :, cols], dst_ref=sib_r.at[at, :, cols],
            send_sem=sib_ss.at[at, which], recv_sem=sib_rs.at[at, which],
            device_id=sibling, device_id_type=MESH,
        )

    def col_copy(at, side, dist, to, which):
        cols = OUTS[which]
        return pltpu.make_async_remote_copy(
            src_ref=col_s.at[at, :, cols], dst_ref=col_r.at[side, dist - 1, :, cols],
            send_sem=col_ss.at[side, dist - 1, which], recv_sem=col_rs.at[side, dist - 1, which],
            device_id=(row, to * 2 + core), device_id_type=MESH,
        )

    def fin_copy(which):
        cols = OUTS[which]
        return pltpu.make_async_remote_copy(
            src_ref=fin_s.at[:, cols], dst_ref=fin_r.at[:, cols], send_sem=fin_ss.at[which],
            recv_sem=fin_rs.at[which], device_id=same_core(1), device_id_type=MESH,
        )

    def send_x(at, off):
        owner = (z + off + 4 * core) % NZ
        to_x, side = owner // 2, owner % 2
        for which in range(2):
            cols = OUTS[which]
            sib_copy(at, which).wait_recv()

            @pl.when(to_x == x)
            def _():
                acc[side, :, cols] = oi[at, core, :, cols] + sib_r[at, :, cols]

            @pl.when(to_x != x)
            def _():
                @rows(T)
                def _(r):
                    col_s[at, r, cols] = enc3(oi[at, core, r, cols] + sib_r[at, r, cols])

                col_copy(at, side, (to_x + 4 - x) % 4, to_x * 2 + yh, which).start()

    def reduce_x(off):
        owner = (z + off + 4 * core) % NZ
        side = owner % 2

        @pl.when(owner // 2 == x)
        def _():
            for which in range(2):
                cols = OUTS[which]
                for dist in (1, 3, 2):
                    col_copy(0, side, dist, chip, which).wait_recv()

                @rows(T)
                def _(r):
                    total = (
                        acc[side, r, cols] + dec3(col_r[side, 0, r, cols])
                        + dec3(col_r[side, 1, r, cols]) + dec3(col_r[side, 2, r, cols])
                    )

                    @pl.when(side == yh)
                    def _():
                        (out_ref, ing_ref)[which][r] = total

                    @pl.when(side != yh)
                    def _():
                        fin_s[r, cols] = enc3(total)

                @pl.when(side != yh)
                def _():
                    fin_copy(which).start()

    last_owner = (z + 4 + 4 * core) % NZ

    def last_copy(k, to, which):
        cols = OUTS[which]
        return pltpu.make_async_remote_copy(
            src_ref=col_s.at[7, :, cols], dst_ref=last_r.at[k, :, cols],
            send_sem=last_ss.at[k, which], recv_sem=last_rs.at[k, which],
            device_id=(row, to * 2 + core), device_id_type=MESH,
        )

    last_k = ((last_owner // 2 + 4 - x) % 4) * 2 + (last_owner + yh) % 2

    def send_last():
        for which in range(2):
            cols = OUTS[which]
            sib_copy(7, which).wait_recv()

            @pl.when(last_owner == chip)
            def _():
                (out_ref, ing_ref)[which][...] = oi[7, core, :, cols] + sib_r[7, :, cols]

            @pl.when(last_owner != chip)
            def _():
                @rows(T)
                def _(r):
                    col_s[7, r, cols] = enc3(oi[7, core, r, cols] + sib_r[7, r, cols])

                last_copy(last_k, last_owner, which).start()

    def finish():
        for which in range(2):
            out = (out_ref, ing_ref)[which]
            cols = OUTS[which]

            @pl.when(last_owner == chip)
            def _():
                for k in range(1, 8):
                    last_copy(k, chip, which).wait_recv()

                @rows(T)
                def _(r):
                    total = out[r]
                    for k in range(1, 8):
                        total += dec3(last_r[k, r, cols])
                    out[r] = total

            @pl.when(last_owner != chip)
            def _():
                fin_copy(which).wait_recv()

                @rows(T)
                def _(r):
                    out[r] += dec3(fin_r[r, cols])

    over = (((0,), (0,)), ((), ()))

    def wgrad_down():
        cots = xc[...].reshape(16 * T, D)
        for ref, width, first in ((ga, FA, 0), (gb, FB, FA)):
            hidden = ref[:, :, 0:width].reshape(16 * T, width)
            d_out[first : first + width, :] = lax.dot_general(hidden, cots, over, preferred_element_type=F32)

    def wgrad_in(out, third):
        for ref, width, first in ((ga, FA, 0), (gb, FB, FA)):
            grads = ref[:, :, third * width : (third + 1) * width].reshape(16 * T, width)
            out[:, first : first + width] = dot(ft[...], grads)

    gby = gb.at[mate[0]]
    pltpu.make_async_remote_copy(
        src_ref=gby, dst_ref=gby, send_sem=gby_ss, recv_sem=gby_rs, device_id=mate, device_id_type=MESH
    ).wait_recv()
    for way in range(2):
        gbz_send(way, 0)

    def offs_of(step):
        return (NZ - 1 - step, step + 1)

    for step in range(4):
        for way in range(2):
            gaz_wait(way, step)
            if step < 3:
                gaz_send(way, step + 1)
                gay_send(offs_of(step)[way])
        if step == 3:
            gay_send(4)
        if step == 0:
            gay_wait(0)
            products(0, 0)
        else:
            for way in range(2):
                off = offs_of(step - 1)[way]
                gay_wait(off)
                products(BPOS[off], off)
        if step == 3:
            for way in range(2):
                off = offs_of(2)[way]
                send_x(BPOS[off], off)
            for way in range(2):
                reduce_x(offs_of(1)[way])
        for way in range(2):
            gbz_wait(way, step)
            if step < 3:
                gbz_send(way, step + 1)
        if step == 0:
            send_x(0, 0)
        elif step < 3:
            for way in range(2):
                off = offs_of(step - 1)[way]
                send_x(BPOS[off], off)
            if step == 1:
                reduce_x(0)
            else:
                for way in range(2):
                    reduce_x(offs_of(step - 2)[way])

    gay_wait(4)
    products(7, 4)
    send_last()
    for way in range(2):
        reduce_x(offs_of(2)[way])
    wgrad_down()
    wgrad_in(g_out, 1)
    wgrad_in(u_out, 2)
    finish()

    for copy in sent:
        copy.wait_send()

    @pl.loop(0, NZ)
    def _(at):
        ya_copy(at, 0).wait_send()
        ya_copy(at, 1).wait_send()
        sib_copy(at, 0).wait_send()
        sib_copy(at, 1).wait_send()

    for side in range(2):
        for dist in range(1, 4):
            owner = ((x + dist) % 4) * 2 + side

            @pl.when(owner != last_owner)
            def _():
                for which in range(2):
                    col_copy(0, side, dist, chip, which).wait_send()

    @pl.when(last_owner != chip)
    def _():
        for which in range(2):
            last_copy(last_k, last_owner, which).wait_send()

    @pl.when(last_owner != at_chip(1))
    def _():
        for which in range(2):
            fin_copy(which).wait_send()


def layer(*operands):
    vmem = pltpu.VMEM
    dma = pltpu.SemaphoreType.DMA
    hbm = pl.BlockSpec(memory_space=pl.ANY)
    full = pl.BlockSpec(memory_space=pltpu.VMEM)
    return pl.pallas_call(
        layer_kernel,
        out_shape=(
            vmem((T, D), F32),
            vmem((T, D), F32),
            vmem((D, F), F32),
            vmem((D, F), F32),
            vmem((F, D), F32),
        ),
        in_specs=[hbm] * 5,
        out_specs=(full,) * 5,
        scratch_shapes=[
            vmem((D, F), BF16),
            vmem((D, F), BF16),
            vmem((F, D), BF16),
            vmem((16, T, D), BF16),
            vmem((16, T, D), BF16),
            vmem((D, 16 * T), BF16),
            vmem((NZ, 2 * T, CA), F32),
            vmem((NZ, 2 * T, CB), F32),
            vmem((NZ, T, CA), BF16),
            vmem((NZ, T, CA), BF16),
            vmem((T, CB), BF16),
            vmem((T, CB), BF16),
            vmem((2, 4, T, CA), BF16),
            vmem((2, 4, T, CA), BF16),
            vmem((2, 4, 2 * T, CB), BF16),
            vmem((2, 4, 2 * T, CB), BF16),
            vmem((16, T, CA), BF16),
            vmem((16, T, CB), BF16),
            vmem((NZ, 2, T, 2 * D), F32),
            vmem((NZ, T, 2 * D), F32),
            vmem((NZ, T, 2 * D), BF16),
            vmem((2, 3, T, 2 * D), BF16),
            vmem((2, T, 2 * D), F32),
            vmem((T, 2 * D), BF16),
            vmem((T, 2 * D), BF16),
            vmem((8, T, 2 * D), BF16),
            dma((5,)),
            dma((8,)), dma((8,)), dma((8,)), dma((8,)),
            dma((8,)), dma((8,)), dma((8,)), dma((8,)),
            dma((8, 2)), dma((8, 2)), dma, dma,
            dma((2, 2, 4)), dma((2, 2, 4)), dma((2, 2, 4)), dma((2, 2, 4)),
            dma((2, 4)), dma((2, 4)), dma((8,)), dma((8,)),
            dma((2, 4)), dma((2, 4)), dma, dma,
            dma((8, 2)), dma((8, 2)), dma((2, 3, 2)), dma((2, 3, 2)), dma((2,)), dma((2,)), dma((8, 2)), dma((8, 2)),
        ],
        compiler_params=pltpu.CompilerParams(
            collective_id=0, has_side_effects=True, vmem_limit_bytes=48 * 1024 * 1024
        ),
        name="layer",
    )(*[pltpu.with_memory_space_constraint(operand, pltpu.HBM) for operand in operands])


def store_kernel(*refs):
    sources, targets, sem = refs[:5], refs[5:10], refs[10]
    copies = []
    for n in (2, 3, 4, 0, 1):
        count = 4 if n >= 2 else 1
        size = sources[n].shape[0] // count
        for part in range(count):
            at = pl.ds(part * size, size)
            copies.append(pltpu.make_async_copy(sources[n].at[at], targets[n].at[at], sem.at[n, part]))
            copies[-1].start()
    for copy in copies:
        copy.wait()


def store(*arrays):
    return pl.pallas_call(
        store_kernel,
        out_shape=tuple(pltpu.HBM(array.shape, array.dtype) for array in arrays),
        in_specs=[pl.BlockSpec(memory_space=pltpu.VMEM)] * 5,
        out_specs=[pl.BlockSpec(memory_space=pl.ANY)] * 5,
        scratch_shapes=[pltpu.SemaphoreType.DMA((5, 4))],
        compiler_params=pltpu.CompilerParams(vmem_limit_bytes=4 * 1024 * 1024),
        name="store",
    )(*[pltpu.with_memory_space_constraint(array, pltpu.VMEM) for array in arrays])


def body(features, gate_weight, up_weight, down_weight, cotangent):
    return store(*layer(features, gate_weight, up_weight, down_weight, cotangent))


def solution(mesh):
    in_specs = (P("col", "row"), P("row", "col"), P("row", "col"), P("col", "row"), P("col", "row"))
    out_specs = (
        P("col", "row"),
        P("col", "row"),
        P("row", "col"),
        P("row", "col"),
        P("col", "row"),
    )
    return jax.shard_map(body, mesh=mesh, in_specs=in_specs, out_specs=out_specs, check_vma=False)
```

```python
import jax
import jax.numpy as jnp
from jax import lax
from jax.experimental import pallas as pl
from jax.experimental.pallas import tpu as pltpu
from jax.sharding import PartitionSpec as P

MESH = pl.DeviceIdType.MESH
F32, BF16 = jnp.float32, jnp.bfloat16
NZ = 8
T = 48
D = 512
FA, FB = 512, 384
F = FA + FB
CA, CB = 3 * FA, 3 * FB
HALF = CA // 2
SCALE = 4096.0
CSCALE = 1024.0
SMALL = 2.0**-20
ORDER = (4, 3, 5, 2, 6, 1, 7, 0)
POS = {off: at for at, off in enumerate(ORDER)}
BACK = (0, 1, 7, 2, 6, 3, 5, 4)
BPOS = {off: at for at, off in enumerate(BACK)}


def enc5(value):
    value = value * SCALE
    square = value * value
    return (square * square * value).astype(BF16)


def dec5(code):
    code = code.astype(F32)
    root = jnp.exp2(jnp.log2(jnp.abs(code)) * 0.2) * (1.0 / SCALE)
    return jnp.where(code < 0, -root, root)


def enc3(value):
    value = value * CSCALE
    size = jnp.abs(value)
    return (value * jnp.where(size < SMALL, SMALL * SMALL, value * value)).astype(BF16)


def dec3(code):
    code = code.astype(F32)
    size = jnp.abs(code)
    root = jnp.exp2(jnp.log2(size) * (1.0 / 3.0))
    root = jnp.where(size < SMALL**3, size * (1.0 / SMALL**2), root) * (1.0 / CSCALE)
    return jnp.where(code < 0, -root, root)


def dot(left, right):
    return jnp.dot(left, right, preferred_element_type=F32)


def dot_t(left, right):
    return lax.dot_general(left, right, (((1,), (1,)), ((), ())), preferred_element_type=F32)


def rows(count, step=16):
    def run(fn):
        @pl.loop(0, count // step)
        def _(i):
            fn(pl.ds(pl.multiple_of(i * step, step), step))

    return run


def layer_kernel(
    x_hbm, g_hbm, u_hbm, d_hbm, c_hbm,
    out_ref, ing_ref, g_out, u_out, d_out,
    g_w, u_w, d_w, xf, xc, ft, pa, pb, ya_s, ya_r, yb_s, yb_r, za_s, za_r, zb_s, zb_r,
    ga, gb, oi, sib_r, col_s, col_r, acc, fin_s, fin_r, last_r,
    load_sem, f_ss, f_rs, c_ss, c_rs, ff_ss, ff_rs, cf_ss, cf_rs, ya_ss, ya_rs, yb_ss, yb_rs,
    za_ss, za_rs, zb_ss, zb_rs, gaz_ss, gaz_rs, gay_ss, gay_rs, gbz_ss, gbz_rs, gby_ss, gby_rs,
    sib_ss, sib_rs, col_ss, col_rs, fin_ss, fin_rs, last_ss, last_rs,
):
    row, col = lax.axis_index("row"), lax.axis_index("col")
    z, yl = row // 2, row % 2
    chip, core = col // 2, col % 2
    x, yh = chip // 2, chip % 2

    def at_chip(k):
        return ((x + k // 2) % 4) * 2 + (yh + k % 2) % 2

    def from_chip(k):
        return ((x + 4 - k // 2) % 4) * 2 + (yh + k % 2) % 2

    def place(of_chip):
        return ((of_chip + 4 * core) % 8) * 2 + core

    up_z = ((z + 1) % NZ) * 2 + yl
    down_z = ((z + NZ - 1) % NZ) * 2 + yl
    mate = (z * 2 + 1 - yl, col)
    sibling = (row, chip * 2 + 1 - core)
    ring = ((up_z, col), (down_z, col))

    def send(src, dst, ss, rs, to):
        copy = pltpu.make_async_remote_copy(
            src_ref=src, dst_ref=dst, send_sem=ss, recv_sem=rs, device_id=to, device_id_type=MESH
        )
        copy.start()
        return copy

    sent = []

    loads = [
        pltpu.make_async_copy(x_hbm, xf.at[place(chip)], load_sem.at[0]),
        pltpu.make_async_copy(c_hbm, xc.at[place(chip)], load_sem.at[1]),
        pltpu.make_async_copy(g_hbm, g_w, load_sem.at[2]),
        pltpu.make_async_copy(u_hbm, u_w, load_sem.at[3]),
        pltpu.make_async_copy(d_hbm, d_w, load_sem.at[4]),
    ]
    for copy in loads:
        copy.start()

    barrier = pltpu.get_barrier_semaphore()
    for k in range(1, 8):
        pl.semaphore_signal(barrier, inc=1, device_id=(row, from_chip(k) * 2 + core), device_id_type=MESH)
    for to in (sibling, mate, ring[0], ring[1]):
        pl.semaphore_signal(barrier, inc=1, device_id=to, device_id_type=MESH)
    pl.semaphore_wait(barrier, 11)
    loads[0].wait()
    loads[1].wait()

    def arrival(ref, ss, rs):
        return pltpu.make_async_remote_copy(
            src_ref=ref, dst_ref=ref, send_sem=ss, recv_sem=rs, device_id=mate, device_id_type=MESH
        )

    def same_core(k):
        return (row, at_chip(k) * 2 + core)

    mine_f, mine_c = xf.at[place(chip)], xc.at[place(chip)]
    for k in (4, 5, 2, 6, 3, 7, 1):
        sent.append(send(mine_f, mine_f, f_ss.at[k], f_rs.at[k], same_core(k)))
    sent.append(send(mine_f, mine_f, ff_ss.at[0], ff_rs.at[0], sibling))
    for k in (1, 4, 2, 6):
        sent.append(send(mine_c, mine_c, c_ss.at[k], c_rs.at[k], same_core(k)))
    sent.append(send(mine_c, mine_c, cf_ss.at[0], cf_rs.at[0], sibling))

    def pass_on(ref, ss, rs, to_ss, to_rs, k):
        part = ref.at[place(from_chip(k))]
        arrival(part, ss.at[k], rs.at[k]).wait_recv()
        sent.append(send(part, part, to_ss.at[k], to_rs.at[k], sibling))

    for k in (1, 2, 6, 3, 7, 4, 5):
        pass_on(xf, f_ss, f_rs, ff_ss, ff_rs, k)
    pass_on(xc, c_ss, c_rs, cf_ss, cf_rs, 1)
    partner = xc.at[place(from_chip(1))]
    for k in (5, 3, 7):
        sent.append(send(partner, partner, c_ss.at[k], c_rs.at[k], same_core(k - 1)))
    for copy in loads[2:]:
        copy.wait()
    for k in range(8):
        arrival(mine_f, ff_ss.at[k], ff_rs.at[k]).wait_recv()

    def tokens(ref, off):
        piece = (z + off) % NZ
        return jnp.concatenate([ref[2 * piece + yl], ref[2 * piece + 1 - yl]], axis=0)

    def mates(r):
        return pl.ds(pl.multiple_of(r.start + T, 16), 16)

    def partial_gu(at, off):
        feats = tokens(xf, off)
        pa[at, :, 0:FA] = dot(feats, g_w[:, 0:FA])
        pa[at, :, FA : 2 * FA] = dot(feats, u_w[:, 0:FA])
        pb[at, :, 0:FB] = dot(feats, g_w[:, FA:F])
        pb[at, :, FB : 2 * FB] = dot(feats, u_w[:, FA:F])

        @rows(T)
        def _(r):
            ya_s[at, r, 0 : 2 * FA] = enc5(pa[at, mates(r), 0 : 2 * FA])

    def partial_h(at, off):
        cots = tokens(xc, off)
        pa[at, :, 2 * FA : CA] = dot_t(cots, d_w[0:FA, :])
        pb[at, :, 2 * FB : CB] = dot_t(cots, d_w[FA:F, :])

        @rows(T)
        def _(r):
            ya_s[at, r, 2 * FA : CA] = enc5(pa[at, mates(r), 2 * FA : CA])

    A_COLS = ((0, 2 * FA), (2 * FA, FA))
    B_COLS = ((0, 2 * FB), (2 * FB, FB))

    def ya_copy(at, which):
        cols = pl.ds(*A_COLS[which])
        return pltpu.make_async_remote_copy(
            src_ref=ya_s.at[at, :, cols], dst_ref=ya_r.at[at, :, cols],
            send_sem=ya_ss.at[at, which], recv_sem=ya_rs.at[at, which],
            device_id=mate, device_id_type=MESH,
        )

    def half(which, way):
        first, width = A_COLS[which]
        return pl.ds(first + way * (width // 2), width // 2)

    def za_copy(which, way, step):
        cols = pl.ds(*A_COLS[which]) if step else half(which, way)
        part = (way, step, slice(None), cols)
        return pltpu.make_async_remote_copy(
            src_ref=za_s.at[part], dst_ref=za_r.at[part],
            send_sem=za_ss.at[which, way, step], recv_sem=za_rs.at[which, way, step],
            device_id=ring[way], device_id_type=MESH,
        )

    def zb_copy(which, way, step):
        tok = slice(None) if step else pl.ds(way * T, T)
        part = (way, step, tok, pl.ds(*B_COLS[which]))
        return pltpu.make_async_remote_copy(
            src_ref=zb_s.at[part], dst_ref=zb_r.at[part],
            send_sem=zb_ss.at[which, way, step], recv_sem=zb_rs.at[which, way, step],
            device_id=ring[way], device_id_type=MESH,
        )

    def za_step(which, step):
        if step == 0:
            ya_copy(0, which).wait_recv()
        for way in range(2):
            at = POS[4 - step if way == 0 else 4 + step]
            if step:
                ya_copy(at, which).wait_recv()
                za_copy(which, way, step - 1).wait_recv()
            cols = pl.ds(*A_COLS[which])
            got, rest = half(which, way), half(which, 1 - way)

            @rows(T)
            def _(r):
                if step == 0:
                    za_s[way, 0, r, got] = enc5(pa[at, r, got] + dec5(ya_r[at, r, got]))
                elif step == 1:
                    za_s[way, 1, r, got] = enc5(
                        pa[at, r, got] + dec5(ya_r[at, r, got]) + dec5(za_r[way, 0, r, got])
                    )
                    za_s[way, 1, r, rest] = enc5(pa[at, r, rest] + dec5(ya_r[at, r, rest]))
                else:
                    za_s[way, step, r, cols] = enc5(
                        pa[at, r, cols] + dec5(ya_r[at, r, cols]) + dec5(za_r[way, step - 1, r, cols])
                    )

            copy = za_copy(which, way, step)
            copy.start()
            sent.append(copy)

    def zb_step(which, step):
        for way in range(2):
            at = POS[4 - step if way == 0 else 4 + step]
            if step:
                zb_copy(which, way, step - 1).wait_recv()
            cols = pl.ds(*B_COLS[which])

            def shifted(r, by):
                return pl.ds(pl.multiple_of(r.start + by, 16), 16)

            if step < 2:

                @rows(T)
                def _(r):
                    got, rest = shifted(r, way * T), shifted(r, (1 - way) * T)
                    if step == 0:
                        zb_s[way, 0, got, cols] = enc5(pb[at, got, cols])
                    else:
                        zb_s[way, 1, got, cols] = enc5(pb[at, got, cols] + dec5(zb_r[way, 0, got, cols]))
                        zb_s[way, 1, rest, cols] = enc5(pb[at, rest, cols])
            else:

                @rows(2 * T)
                def _(r):
                    zb_s[way, step, r, cols] = enc5(pb[at, r, cols] + dec5(zb_r[way, step - 1, r, cols]))

            copy = zb_copy(which, way, step)
            copy.start()
            sent.append(copy)

    def off_at(at):
        return jnp.where(at % 2 == 1, 4 - (at + 1) // 2, 4 + at // 2)

    partial_gu(0, 4)
    ya_copy(0, 0).start()
    zb_step(0, 0)

    @pl.loop(1, 3)
    def _(at):
        partial_gu(at, off_at(at))
        ya_copy(at, 0).start()

    @pl.loop(3, NZ)
    def _(at):
        partial_gu(at, off_at(at))

    zb_step(0, 1)
    for k in (2, 6, 4, 3, 7, 5):
        pass_on(xc, c_ss, c_rs, cf_ss, cf_rs, k)
    za_step(0, 0)
    for k in range(8):
        arrival(mine_c, cf_ss.at[k], cf_rs.at[k]).wait_recv()

    partial_h(0, 4)
    ya_copy(0, 1).start()
    zb_step(1, 0)

    @pl.loop(1, 3)
    def _(at):
        partial_h(at, off_at(at))
        ya_copy(at, 1).start()

    @pl.loop(3, NZ)
    def _(at):
        partial_h(at, off_at(at))
        ya_copy(at, 0).start()
        ya_copy(at, 1).start()

    zb_step(0, 2)
    za_step(0, 1)
    zb_step(1, 1)
    za_step(1, 0)
    zb_step(0, 3)
    zb_step(1, 2)
    za_step(1, 1)
    zb_step(1, 3)
    ft[...] = xf[...].reshape(16 * T, D).T
    za_step(0, 2)
    za_step(1, 2)

    for which in range(2):
        for way in range(2):
            zb_copy(which, way, 3).wait_recv()

    @rows(T)
    def _(r):
        r2 = pl.ds(pl.multiple_of(r.start + T, 16), 16)
        yb_s[r] = enc5(pb[7, r2] + dec5(zb_r[0, 3, r2]) + dec5(zb_r[1, 3, r2]))

    yb_move = send(yb_s, yb_r, yb_ss, yb_rs, mate)
    sent.append(yb_move)

    def activate(gate, up, hid):
        sig = jax.nn.sigmoid(gate)
        silu = gate * sig
        return (
            (silu * up).astype(BF16),
            (hid * up * sig * (1.0 + gate * (1.0 - sig))).astype(BF16),
            (hid * silu).astype(BF16),
        )

    za_step(0, 3)
    za_step(1, 3)
    for which in range(2):
        ya_copy(7, which).wait_recv()
        for way in range(2):
            za_copy(which, way, 3).wait_recv()

    @rows(T)
    def _(r):
        def total(first):
            cols = pl.ds(first, FA)
            return pa[7, r, cols] + dec5(ya_r[7, r, cols]) + dec5(za_r[0, 3, r, cols]) + dec5(za_r[1, 3, r, cols])

        hidden, gate_grad, up_grad = activate(total(0), total(FA), total(2 * FA))
        ga[row, r, 0:FA] = hidden
        ga[row, r, FA : 2 * FA] = gate_grad
        ga[row, r, 2 * FA : CA] = up_grad

    def gaz_send(way, step):
        src = ((z + NZ - step) % NZ if way == 0 else (z + step) % NZ) * 2 + yl
        if step < 3:
            part = ga.at[src]
        else:
            part = ga.at[src, :, pl.ds(way * HALF, HALF)]
        copy = send(part, part, gaz_ss.at[way, step], gaz_rs.at[way, step], ring[way])
        sent.append(copy)

    def gaz_wait(way, step):
        src = ((z + NZ - 1 - step) % NZ if way == 0 else (z + step + 1) % NZ) * 2 + yl
        if step < 3:
            part = ga.at[src]
        else:
            part = ga.at[src, :, pl.ds(way * HALF, HALF)]
        pltpu.make_async_remote_copy(
            src_ref=part, dst_ref=part, send_sem=gaz_ss.at[way, step], recv_sem=gaz_rs.at[way, step],
            device_id=mate, device_id_type=MESH,
        ).wait_recv()

    def gay_send(off):
        part = ga.at[((z + off) % NZ) * 2 + yl]
        sent.append(send(part, part, gay_ss.at[off], gay_rs.at[off], mate))

    def gay_wait(off):
        part = ga.at[((z + off) % NZ) * 2 + 1 - yl]
        pltpu.make_async_remote_copy(
            src_ref=part, dst_ref=part, send_sem=gay_ss.at[off], recv_sem=gay_rs.at[off],
            device_id=mate, device_id_type=MESH,
        ).wait_recv()

    def gbz_part(way, step, src):
        if step < 3:
            return gb.at[pl.ds(2 * src, 2)]
        return gb.at[2 * src + way]

    def gbz_send(way, step):
        part = gbz_part(way, step, (z + NZ - step) % NZ if way == 0 else (z + step) % NZ)
        sent.append(send(part, part, gbz_ss.at[way, step], gbz_rs.at[way, step], ring[way]))

    def gbz_wait(way, step):
        part = gbz_part(way, step, (z + NZ - 1 - step) % NZ if way == 0 else (z + step + 1) % NZ)
        pltpu.make_async_remote_copy(
            src_ref=part, dst_ref=part, send_sem=gbz_ss.at[way, step], recv_sem=gbz_rs.at[way, step],
            device_id=mate, device_id_type=MESH,
        ).wait_recv()

    for way in range(2):
        gaz_send(way, 0)
    yb_move.wait_recv()

    @rows(T)
    def _(r):
        def total(first):
            cols = pl.ds(first, FB)
            return (
                pb[7, r, cols] + dec5(zb_r[0, 3, r, cols]) + dec5(zb_r[1, 3, r, cols]) + dec5(yb_r[r, cols])
            )

        hidden, gate_grad, up_grad = activate(total(0), total(FB), total(2 * FB))
        gb[row, r, 0:FB] = hidden
        gb[row, r, FB : 2 * FB] = gate_grad
        gb[row, r, 2 * FB : CB] = up_grad

    part = gb.at[row]
    sent.append(send(part, part, gby_ss, gby_rs, mate))
    gay_send(0)

    def products(at, off):
        piece = (z + off) % NZ
        both = pl.ds(2 * piece, 2)

        def part(ref, first, width):
            return ref[both, :, first : first + width].reshape(2 * T, width)

        outs = dot(part(ga, 0, FA), d_w[0:FA, :]) + dot(part(gb, 0, FB), d_w[FA:F, :])
        oi[at, :, :, 0:D] = outs.reshape(2, T, D)
        sib_copy(at, 0).start()
        grads = (
            dot_t(part(ga, FA, FA), g_w[:, 0:FA])
            + dot_t(part(ga, 2 * FA, FA), u_w[:, 0:FA])
            + dot_t(part(gb, FB, FB), g_w[:, FA:F])
            + dot_t(part(gb, 2 * FB, FB), u_w[:, FA:F])
        )
        oi[at, :, :, D : 2 * D] = grads.reshape(2, T, D)
        sib_copy(at, 1).start()

    OUTS = (pl.ds(0, D), pl.ds(D, D))

    def sib_copy(at, which):
        cols = OUTS[which]
        return pltpu.make_async_remote_copy(
            src_ref=oi.at[at, 1 - core, :, cols], dst_ref=sib_r.at[at, :, cols],
            send_sem=sib_ss.at[at, which], recv_sem=sib_rs.at[at, which],
            device_id=sibling, device_id_type=MESH,
        )

    def col_copy(at, side, dist, to, which):
        cols = OUTS[which]
        return pltpu.make_async_remote_copy(
            src_ref=col_s.at[at, :, cols], dst_ref=col_r.at[side, dist - 1, :, cols],
            send_sem=col_ss.at[side, dist - 1, which], recv_sem=col_rs.at[side, dist - 1, which],
            device_id=(row, to * 2 + core), device_id_type=MESH,
        )

    def fin_copy(which):
        cols = OUTS[which]
        return pltpu.make_async_remote_copy(
            src_ref=fin_s.at[:, cols], dst_ref=fin_r.at[:, cols], send_sem=fin_ss.at[which],
            recv_sem=fin_rs.at[which], device_id=same_core(1), device_id_type=MESH,
        )

    def send_x(at, off):
        owner = (z + off + 4 * core) % NZ
        to_x, side = owner // 2, owner % 2
        for which in range(2):
            cols = OUTS[which]
            sib_copy(at, which).wait_recv()

            @pl.when(to_x == x)
            def _():
                acc[side, :, cols] = oi[at, core, :, cols] + sib_r[at, :, cols]

            @pl.when(to_x != x)
            def _():
                @rows(T)
                def _(r):
                    col_s[at, r, cols] = enc3(oi[at, core, r, cols] + sib_r[at, r, cols])

                col_copy(at, side, (to_x + 4 - x) % 4, to_x * 2 + yh, which).start()

    def reduce_x(off):
        owner = (z + off + 4 * core) % NZ
        side = owner % 2

        @pl.when(owner // 2 == x)
        def _():
            for which in range(2):
                cols = OUTS[which]
                for dist in (1, 3, 2):
                    col_copy(0, side, dist, chip, which).wait_recv()

                @rows(T)
                def _(r):
                    total = (
                        acc[side, r, cols] + dec3(col_r[side, 0, r, cols])
                        + dec3(col_r[side, 1, r, cols]) + dec3(col_r[side, 2, r, cols])
                    )

                    @pl.when(side == yh)
                    def _():
                        (out_ref, ing_ref)[which][r] = total

                    @pl.when(side != yh)
                    def _():
                        fin_s[r, cols] = enc3(total)

                @pl.when(side != yh)
                def _():
                    fin_copy(which).start()

    last_owner = (z + 4 + 4 * core) % NZ

    def last_copy(k, to, which):
        cols = OUTS[which]
        return pltpu.make_async_remote_copy(
            src_ref=col_s.at[7, :, cols], dst_ref=last_r.at[k, :, cols],
            send_sem=last_ss.at[k, which], recv_sem=last_rs.at[k, which],
            device_id=(row, to * 2 + core), device_id_type=MESH,
        )

    last_k = ((last_owner // 2 + 4 - x) % 4) * 2 + (last_owner + yh) % 2

    def send_last():
        for which in range(2):
            cols = OUTS[which]
            sib_copy(7, which).wait_recv()

            @pl.when(last_owner == chip)
            def _():
                (out_ref, ing_ref)[which][...] = oi[7, core, :, cols] + sib_r[7, :, cols]

            @pl.when(last_owner != chip)
            def _():
                @rows(T)
                def _(r):
                    col_s[7, r, cols] = enc3(oi[7, core, r, cols] + sib_r[7, r, cols])

                last_copy(last_k, last_owner, which).start()

    def finish():
        for which in range(2):
            out = (out_ref, ing_ref)[which]
            cols = OUTS[which]

            @pl.when(last_owner == chip)
            def _():
                for k in range(1, 8):
                    last_copy(k, chip, which).wait_recv()

                @rows(T)
                def _(r):
                    total = out[r]
                    for k in range(1, 8):
                        total += dec3(last_r[k, r, cols])
                    out[r] = total

            @pl.when(last_owner != chip)
            def _():
                fin_copy(which).wait_recv()

                @rows(T)
                def _(r):
                    out[r] += dec3(fin_r[r, cols])

    over = (((0,), (0,)), ((), ()))

    def wgrad_down():
        cots = xc[...].reshape(16 * T, D)
        for ref, width, first in ((ga, FA, 0), (gb, FB, FA)):
            hidden = ref[:, :, 0:width].reshape(16 * T, width)
            d_out[first : first + width, :] = lax.dot_general(hidden, cots, over, preferred_element_type=F32)

    def wgrad_in(out, third):
        for ref, width, first in ((ga, FA, 0), (gb, FB, FA)):
            grads = ref[:, :, third * width : (third + 1) * width].reshape(16 * T, width)
            out[:, first : first + width] = dot(ft[...], grads)

    gby = gb.at[mate[0]]
    pltpu.make_async_remote_copy(
        src_ref=gby, dst_ref=gby, send_sem=gby_ss, recv_sem=gby_rs, device_id=mate, device_id_type=MESH
    ).wait_recv()
    for way in range(2):
        gbz_send(way, 0)

    def offs_of(step):
        return (NZ - 1 - step, step + 1)

    for step in range(4):
        for way in range(2):
            gaz_wait(way, step)
            if step < 3:
                gaz_send(way, step + 1)
                gay_send(offs_of(step)[way])
        if step == 3:
            gay_send(4)
        if step == 0:
            gay_wait(0)
            products(0, 0)
        else:
            for way in range(2):
                off = offs_of(step - 1)[way]
                gay_wait(off)
                products(BPOS[off], off)
        if step == 3:
            for way in range(2):
                off = offs_of(2)[way]
                send_x(BPOS[off], off)
            for way in range(2):
                reduce_x(offs_of(1)[way])
        for way in range(2):
            gbz_wait(way, step)
            if step < 3:
                gbz_send(way, step + 1)
        if step == 0:
            send_x(0, 0)
        elif step < 3:
            for way in range(2):
                off = offs_of(step - 1)[way]
                send_x(BPOS[off], off)
            if step == 1:
                reduce_x(0)
            else:
                for way in range(2):
                    reduce_x(offs_of(step - 2)[way])

    gay_wait(4)
    products(7, 4)
    send_last()
    for way in range(2):
        reduce_x(offs_of(2)[way])
    wgrad_down()
    wgrad_in(g_out, 1)
    wgrad_in(u_out, 2)
    finish()

    for copy in sent:
        copy.wait_send()

    @pl.loop(0, NZ)
    def _(at):
        ya_copy(at, 0).wait_send()
        ya_copy(at, 1).wait_send()
        sib_copy(at, 0).wait_send()
        sib_copy(at, 1).wait_send()

    for side in range(2):
        for dist in range(1, 4):
            owner = ((x + dist) % 4) * 2 + side

            @pl.when(owner != last_owner)
            def _():
                for which in range(2):
                    col_copy(0, side, dist, chip, which).wait_send()

    @pl.when(last_owner != chip)
    def _():
        for which in range(2):
            last_copy(last_k, last_owner, which).wait_send()

    @pl.when(last_owner != at_chip(1))
    def _():
        for which in range(2):
            fin_copy(which).wait_send()


def layer(*operands):
    vmem = pltpu.VMEM
    dma = pltpu.SemaphoreType.DMA
    hbm = pl.BlockSpec(memory_space=pl.ANY)
    full = pl.BlockSpec(memory_space=pltpu.VMEM)
    return pl.pallas_call(
        layer_kernel,
        out_shape=(
            vmem((T, D), F32),
            vmem((T, D), F32),
            vmem((D, F), F32),
            vmem((D, F), F32),
            vmem((F, D), F32),
        ),
        in_specs=[hbm] * 5,
        out_specs=(full,) * 5,
        scratch_shapes=[
            vmem((D, F), BF16),
            vmem((D, F), BF16),
            vmem((F, D), BF16),
            vmem((16, T, D), BF16),
            vmem((16, T, D), BF16),
            vmem((D, 16 * T), BF16),
            vmem((NZ, 2 * T, CA), F32),
            vmem((NZ, 2 * T, CB), F32),
            vmem((NZ, T, CA), BF16),
            vmem((NZ, T, CA), BF16),
            vmem((T, CB), BF16),
            vmem((T, CB), BF16),
            vmem((2, 4, T, CA), BF16),
            vmem((2, 4, T, CA), BF16),
            vmem((2, 4, 2 * T, CB), BF16),
            vmem((2, 4, 2 * T, CB), BF16),
            vmem((16, T, CA), BF16),
            vmem((16, T, CB), BF16),
            vmem((NZ, 2, T, 2 * D), F32),
            vmem((NZ, T, 2 * D), F32),
            vmem((NZ, T, 2 * D), BF16),
            vmem((2, 3, T, 2 * D), BF16),
            vmem((2, T, 2 * D), F32),
            vmem((T, 2 * D), BF16),
            vmem((T, 2 * D), BF16),
            vmem((8, T, 2 * D), BF16),
            dma((5,)),
            dma((8,)), dma((8,)), dma((8,)), dma((8,)),
            dma((8,)), dma((8,)), dma((8,)), dma((8,)),
            dma((8, 2)), dma((8, 2)), dma, dma,
            dma((2, 2, 4)), dma((2, 2, 4)), dma((2, 2, 4)), dma((2, 2, 4)),
            dma((2, 4)), dma((2, 4)), dma((8,)), dma((8,)),
            dma((2, 4)), dma((2, 4)), dma, dma,
            dma((8, 2)), dma((8, 2)), dma((2, 3, 2)), dma((2, 3, 2)), dma((2,)), dma((2,)), dma((8, 2)), dma((8, 2)),
        ],
        compiler_params=pltpu.CompilerParams(
            collective_id=0, has_side_effects=True, vmem_limit_bytes=48 * 1024 * 1024
        ),
        name="layer",
    )(*[pltpu.with_memory_space_constraint(operand, pltpu.HBM) for operand in operands])


def store_kernel(*refs):
    sources, targets, sem = refs[:5], refs[5:10], refs[10]
    copies = []
    for n in (2, 3, 4, 0, 1):
        count = 4 if n >= 2 else 1
        size = sources[n].shape[0] // count
        for part in range(count):
            at = pl.ds(part * size, size)
            copies.append(pltpu.make_async_copy(sources[n].at[at], targets[n].at[at], sem.at[n, part]))
            copies[-1].start()
    for copy in copies:
        copy.wait()


def store(*arrays):
    return pl.pallas_call(
        store_kernel,
        out_shape=tuple(pltpu.HBM(array.shape, array.dtype) for array in arrays),
        in_specs=[pl.BlockSpec(memory_space=pltpu.VMEM)] * 5,
        out_specs=[pl.BlockSpec(memory_space=pl.ANY)] * 5,
        scratch_shapes=[pltpu.SemaphoreType.DMA((5, 4))],
        compiler_params=pltpu.CompilerParams(vmem_limit_bytes=4 * 1024 * 1024),
        name="store",
    )(*[pltpu.with_memory_space_constraint(array, pltpu.VMEM) for array in arrays])


def body(features, gate_weight, up_weight, down_weight, cotangent):
    return store(*layer(features, gate_weight, up_weight, down_weight, cotangent))


def solution(mesh):
    in_specs = (P("col", "row"), P("row", "col"), P("row", "col"), P("col", "row"), P("col", "row"))
    out_specs = (
        P("col", "row"),
        P("col", "row"),
        P("row", "col"),
        P("row", "col"),
        P("col", "row"),
    )
    return jax.shard_map(body, mesh=mesh, in_specs=in_specs, out_specs=out_specs, check_vma=False)
```
